128 devices in a mesh: lat: 16 (over y, z), lon: 8 (over x, core).
Axes of the slice: x: 4, y: 4, z: 4, core: 2. Of those that a mesh axis runs over, the one named last changes fastest.
Arguments:
- coarse_field: bfloat16 [96, 720, 1440], P(None, 'lat', 'lon'), may hold values from -6 to 6
- forward_table: bfloat16 [368, 720, 720], P('lon', 'lat'), as said below
- degree_mixing_weight: bfloat16 [720, 96, 192], P('lat'), may hold values from -0.4375 to 0.4375
- synthesis_weight_table: bfloat16 [368, 720, 1024], P('lon', None, 'lat'), as said below
Outputs:
- upsampled: bfloat16 [96, 1024, 3600], P(None, 'lat', 'lon')
The draws below stay inside these ranges and needn't reach their ends.
Inputs may be any that keep to these rules, and one draw needn't show every extreme that they name: forward_table[m, l, q] is zero wherever l < m. synthesis_weight_table[m, l, o] is zero wherever l < m.
All inputs are finite; a program needn't handle non-finite values.
Results may differ from the reference program's by a relative error of at most 0.012.
Values may be sent and summed in bfloat16 or wider, within the bound.
No kernel may reach another device: no remote copies, remote signals or barrier semaphores. Data moves between devices by JAX's collectives and lax.ppermute only.
A program may use at most 128 MiB of HBM per device.

```python
import math
import jax
import jax.numpy as jnp
from jax import lax

CHAN = 96
DEGREES = 720
KEPT_ORDERS = 368
INPUT_LATITUDES = 720
LON_IN = 1440
LON_OUT = 3600
OUT_LAT = 1024


def triangle_values(key, shape):
    values = jnp.clip(jax.random.normal(key, shape, jnp.float32), -4.0, 4.0)
    upper_mask = jnp.arange(shape[1])[None, :, None] >= jnp.arange(shape[0])[:, None, None]
    return values * upper_mask.astype(jnp.float32)


def draw_forward_table(key, part):
    key = jax.random.fold_in(key, 11)
    values = triangle_values(key, (KEPT_ORDERS, DEGREES, INPUT_LATITUDES))
    return (values * INPUT_LATITUDES ** (-0.5)).astype(jnp.bfloat16)


def draw_synthesis_weight_table(key, part):
    key = jax.random.fold_in(key, 12)
    values = triangle_values(key, (KEPT_ORDERS, DEGREES, OUT_LAT))
    return (values * DEGREES ** (-0.5)).astype(jnp.bfloat16)


def steps_of(rng, dims, split, low, high):
    level, own = 1.0, jax.random.fold_in(rng, 6)
    for dim, shards_of in split:
        steps = jnp.exp(jax.random.uniform(jax.random.fold_in(own, dim), (shards_of,), jnp.float32, low / len(split), high / len(split)))
        level = level * jnp.repeat(steps, dims[dim] // shards_of).reshape([-1 if axis == dim else 1 for axis in range(len(dims))])
    return level


def gaussian(stream_key, dims, width, reach, split=(), kind=jnp.bfloat16):
    entries = width * jax.random.normal(stream_key, dims, jnp.float32)
    if split:
        entries = entries * steps_of(stream_key, dims, split, -0.22, 0.18)
    return jnp.clip(entries, -reach, reach).astype(kind)


def setup_inputs(seed: int = 0) -> dict:
    key_of = jax.random.split(jax.random.key(seed), 5)
    return {
        "coarse_field": gaussian(key_of[0], (CHAN, INPUT_LATITUDES, LON_IN), 1.0, 6.0, ((1, 16), (2, 8))),
        "forward_table": draw_forward_table(jax.random.fold_in(key_of[4], 71), 0),
        "degree_mixing_weight": gaussian(key_of[2], (DEGREES, CHAN, 2 * CHAN), (2 * CHAN) ** -0.5, 0.4375, ((0, 16),)),
        "synthesis_weight_table": draw_synthesis_weight_table(jax.random.fold_in(key_of[4], 71), 0),
    }


def phase_table(order_ids, points, modulus, factor):
    phases = (order_ids[:, None] * points[None, :]) % modulus
    angles = (2.0 * math.pi / modulus) * phases.astype(jnp.float32)
    return jnp.stack([jnp.cos(angles) * factor, -jnp.sin(angles) * factor], axis=1)


def reference(coarse_field, forward_table, degree_mixing_weight, synthesis_weight_table):
    order_ids = jnp.arange(KEPT_ORDERS, dtype=jnp.int32)
    analysis = phase_table(order_ids, jnp.arange(LON_IN, dtype=jnp.int32), LON_IN, LON_IN ** -0.5)
    analysis = jnp.transpose(analysis, (2, 0, 1)).reshape(LON_IN, 2 * KEPT_ORDERS).astype(jnp.bfloat16)
    spectrum = jnp.dot(coarse_field.reshape(CHAN * INPUT_LATITUDES, LON_IN), analysis, preferred_element_type=jnp.float32).astype(jnp.bfloat16)
    per_order_values = jnp.transpose(spectrum.reshape(CHAN, INPUT_LATITUDES, KEPT_ORDERS, 2), (2, 1, 0, 3)).reshape(KEPT_ORDERS, INPUT_LATITUDES, 2 * CHAN)

    def analyse(operands):
        return jnp.dot(operands[0], operands[1], preferred_element_type=jnp.float32).astype(jnp.bfloat16)

    coefficients = lax.map(analyse, (forward_table, per_order_values))
    weights32 = degree_mixing_weight.astype(jnp.float32)

    def mix_single_order(block):
        real_imaginary_pair = block.reshape(DEGREES, CHAN, 2).astype(jnp.float32)
        with_real = jnp.einsum('lc,lco->lo', real_imaginary_pair[:, :, 0], weights32)
        with_imag = jnp.einsum('lc,lco->lo', real_imaginary_pair[:, :, 1], weights32)
        real_out = with_real[:, :CHAN] - with_imag[:, CHAN:]
        imag_out = with_real[:, CHAN:] + with_imag[:, :CHAN]
        return jnp.stack([real_out, imag_out], axis=-1).reshape(DEGREES, 2 * CHAN).astype(jnp.bfloat16)

    mixed_coef = lax.map(mix_single_order, coefficients)

    def synthesise(operands):
        return jnp.dot(operands[0].T, operands[1], preferred_element_type=jnp.float32).astype(jnp.bfloat16)

    grid_orders = lax.map(synthesise, (synthesis_weight_table, mixed_coef))
    synth_tab = phase_table(order_ids, jnp.arange(LON_OUT, dtype=jnp.int32), LON_OUT, KEPT_ORDERS ** -0.5)
    synth_tab = synth_tab.reshape(2 * KEPT_ORDERS, LON_OUT).astype(jnp.bfloat16)
    per_channel = jnp.transpose(grid_orders.reshape(KEPT_ORDERS, OUT_LAT, CHAN, 2), (2, 1, 0, 3)).reshape(CHAN, OUT_LAT, 2 * KEPT_ORDERS)

    def synthesise_fine_grid(channel_rows):
        return jnp.dot(channel_rows, synth_tab, preferred_element_type=jnp.float32).astype(jnp.bfloat16)

    return lax.map(synthesise_fine_grid, per_channel)
```

```python
import math

import jax
import jax.numpy as jnp
from jax import lax
from jax.sharding import PartitionSpec as P

CHAN = 96
KEPT_ORDERS = 368
LON_IN = 1440
LON_OUT = 3600
LATS = 16
LONS = 8
OWN = 46
SLOTS = 48
EACH = 3
ROWS = 45
QPAD = 48
QEACH = 6
BF = jnp.bfloat16


def waves(order_ids, valid, points, modulus, factor):
    phases = order_ids * points % modulus
    angles = 2.0 * math.pi / modulus * phases.astype(jnp.float32)
    scale = jnp.where(valid, factor, 0.0)
    return (jnp.cos(angles) * scale).astype(BF), (-jnp.sin(angles) * scale).astype(BF)


def swap(x, axis):
    return lax.all_to_all(x, axis, split_axis=0, concat_axis=0, tiled=True)


def local(coarse_field, forward_table, degree_mixing_weight, synthesis_weight_table):
    ftab = jnp.pad(forward_table, ((0, SLOTS - OWN), (0, 0), (0, 0)))
    ftab = swap(ftab.reshape(LATS, EACH, ROWS, 720), "lat")
    wtab = jnp.transpose(synthesis_weight_table, (0, 2, 1))
    wtab = jnp.pad(wtab, ((0, SLOTS - OWN), (0, 0), (0, 0)))
    wtab = swap(wtab.reshape(LATS, EACH, 64, 720), "lat")

    field = jnp.pad(jnp.transpose(coarse_field, (1, 2, 0)), ((0, QPAD - ROWS), (0, 0), (0, 0)))
    field = swap(field.reshape(LONS, QEACH, 180, CHAN), "lon")

    a = jnp.arange(LATS * LONS * EACH, dtype=jnp.int32)
    slot = (a // (LONS * EACH)) * EACH + a % EACH
    column = (a // EACH) % LONS
    valid = (slot < OWN)[:, None]
    ids = (column * OWN + jnp.minimum(slot, OWN - 1))[:, None]
    points = jnp.arange(LON_IN, dtype=jnp.int32)[None, :]
    cos_in, sin_in = waves(ids, valid, points, LON_IN, LON_IN ** (-0.5))
    field = jnp.transpose(field, (1, 0, 2, 3)).reshape(QEACH, LON_IN, CHAN)
    parts = [
        jnp.einsum("np,qpc->nqc", t, field, preferred_element_type=jnp.float32).astype(BF)
        for t in (cos_in, sin_in)
    ]
    spectrum = jnp.concatenate(parts, axis=-1)
    spectrum = spectrum.reshape(LATS * LONS, EACH, QEACH, 2 * CHAN)
    spectrum = swap(spectrum, ("lat", "lon")).reshape(LATS, LONS, EACH, QEACH, 2 * CHAN)
    spectrum = jnp.transpose(spectrum, (2, 0, 1, 3, 4)).reshape(EACH, LATS, QPAD, 2 * CHAN)
    spectrum = spectrum[:, :, :ROWS].reshape(EACH, 720, 2 * CHAN)

    coef = jnp.einsum("ajlq,jqn->ajln", ftab, spectrum, preferred_element_type=jnp.float32)
    coef = swap(coef.astype(BF), "lat").reshape(SLOTS, ROWS, 2 * CHAN)

    w = degree_mixing_weight
    turned = jnp.concatenate([-w[..., CHAN:], w[..., :CHAN]], axis=-1)
    both = jnp.concatenate([w, turned], axis=1)
    mixed = jnp.einsum("mlt,ltu->mlu", coef, both, preferred_element_type=jnp.float32)
    mixed = swap(mixed.astype(BF).reshape(LATS, EACH, ROWS, 2 * CHAN), "lat")
    mixed = jnp.transpose(mixed, (1, 0, 2, 3)).reshape(EACH, 720, 2 * CHAN)

    rows = jnp.einsum("ajol,jln->ajon", wtab, mixed, preferred_element_type=jnp.float32)
    rows = swap(rows.astype(BF), "lat").reshape(SLOTS, 64, 2, CHAN)

    every = lax.all_gather(rows, "lon", axis=0, tiled=True)
    b = jnp.arange(LONS * SLOTS, dtype=jnp.int32)
    slot = b % SLOTS
    ids = ((b // SLOTS) * OWN + jnp.minimum(slot, OWN - 1))[:, None]
    points = (lax.axis_index("lon") * 450 + jnp.arange(450, dtype=jnp.int32))[None, :]
    cos_out, sin_out = waves(ids, (slot < OWN)[:, None], points, LON_OUT, KEPT_ORDERS ** (-0.5))
    table = jnp.stack([cos_out, sin_out], axis=1)
    out = jnp.einsum("norc,nrp->cop", every, table, preferred_element_type=jnp.float32)
    return out.astype(BF)


def solution(mesh):
    in_specs = (
        P(None, "lat", "lon"),
        P("lon", "lat", None),
        P("lat", None, None),
        P("lon", None, "lat"),
    )
    out_specs = P(None, "lat", "lon")
    return jax.shard_map(local, mesh=mesh, in_specs=in_specs, out_specs=out_specs, check_vma=False)
```

```python
import math

import jax
import jax.numpy as jnp
from jax import lax
from jax.experimental import pallas as pl
from jax.experimental.pallas import tpu as pltpu
from jax.sharding import PartitionSpec as P

CHAN = 96
KEPT_ORDERS = 368
LON_IN = 1440
LON_OUT = 3600
LATS = 16
LONS = 8
OWN = 46
SLOTS = 48
EACH = 3
ROWS = 45
QPAD = 48
PAIRS = 23
OUT_ROWS = 64
OUT_COLS = 450
WIDE = 512
LANES = 128
STEP = 16
VMEM = 56 * 1024 * 1024
QEACH = 6
BF = jnp.bfloat16


def waves(order_ids, valid, points, modulus, factor):
    phases = order_ids * points % modulus
    angles = 2.0 * math.pi / modulus * phases.astype(jnp.float32)
    scale = jnp.where(valid, factor, 0.0)
    return (jnp.cos(angles) * scale).astype(BF), (-jnp.sin(angles) * scale).astype(BF)


def swap(x, axis):
    return lax.all_to_all(x, axis, split_axis=0, concat_axis=0, tiled=True)


def synthesis_kernel(table, mixed, rows):
    m = mixed[:, 0].reshape(LATS * QPAD, 4 * CHAN)
    t = table[:, 0].reshape(2 * OUT_ROWS, LATS * QPAD)
    both = jnp.dot(t, m, preferred_element_type=jnp.float32)
    lane = lax.broadcasted_iota(jnp.int32, (OUT_ROWS, 4 * CHAN), 1)
    rows[0] = jnp.where(lane < 2 * CHAN, both[:OUT_ROWS], both[OUT_ROWS:]).astype(BF)


def synthesise(table, mixed):
    return pl.pallas_call(
        synthesis_kernel,
        grid=(PAIRS,),
        in_specs=[
            pl.BlockSpec((2, 1, OUT_ROWS, LATS * QPAD), lambda p: (0, p, 0, 0)),
            pl.BlockSpec((LATS, 1, QPAD, 4 * CHAN), lambda p: (0, p, 0, 0)),
        ],
        out_specs=pl.BlockSpec((1, OUT_ROWS, 4 * CHAN), lambda p: (p, 0, 0)),
        out_shape=jax.ShapeDtypeStruct((PAIRS, OUT_ROWS, 4 * CHAN), BF),
        compiler_params=pltpu.CompilerParams(vmem_limit_bytes=VMEM),
    )(table, mixed)


def output_kernel(rows, table, out, wide, turned, total):
    count = LONS * PAIRS
    for k in range(3):
        some = rows[:, :, k * LANES : (k + 1) * LANES].astype(jnp.float32)
        wide[k] = some.reshape(count * STEP, LANES)
    for o in range(STEP):
        one = [wide[k, pl.ds(o, count, stride=STEP), :].T for k in range(3)]
        one = jnp.concatenate(one, axis=0).astype(BF)
        for part in range(4):
            turned[part, o * CHAN : (o + 1) * CHAN, :] = one[part * CHAN : (part + 1) * CHAN]
    acc = jnp.dot(turned[0], table[0], preferred_element_type=jnp.float32)
    for part in range(1, 4):
        acc += jnp.dot(turned[part], table[part], preferred_element_type=jnp.float32)
    for k in range(4):
        total[k] = acc[:, k * LANES : (k + 1) * LANES]
    for c in range(CHAN):
        one = [total[k, pl.ds(c, STEP, stride=CHAN), :] for k in range(4)]
        out[c] = jnp.concatenate(one, axis=1)[:, :OUT_COLS].astype(BF)


def to_longitudes(rows, table):
    count = LONS * PAIRS
    return pl.pallas_call(
        output_kernel,
        grid=(OUT_ROWS // STEP,),
        in_specs=[
            pl.BlockSpec((count, STEP, 4 * CHAN), lambda s: (0, s, 0)),
            pl.BlockSpec((4, count, WIDE), lambda s: (0, 0, 0)),
        ],
        out_specs=pl.BlockSpec((CHAN, STEP, OUT_COLS), lambda s: (0, s, 0)),
        out_shape=jax.ShapeDtypeStruct((CHAN, OUT_ROWS, OUT_COLS), BF),
        scratch_shapes=[
            pltpu.VMEM((3, count * STEP, LANES), jnp.float32),
            pltpu.VMEM((4, STEP * CHAN, count), BF),
            pltpu.VMEM((4, STEP * CHAN, LANES), jnp.float32),
        ],
        compiler_params=pltpu.CompilerParams(vmem_limit_bytes=VMEM),
    )(rows, table)


def pick(x, index):
    return lax.dynamic_index_in_dim(x, index, 0, keepdims=False)


def local(coarse_field, forward_table, degree_mixing_weight, synthesis_weight_table):
    ftab = jnp.pad(forward_table, ((0, SLOTS - OWN), (0, 0), (0, 0)))
    ftab = swap(ftab.reshape(LATS, EACH, ROWS, 720), "lat")
    wtab = jnp.transpose(synthesis_weight_table, (0, 2, 1))
    place = jnp.arange(LATS * QPAD, dtype=jnp.int32)
    home = jnp.where(place % QPAD < ROWS, place // QPAD * ROWS + place % QPAD, -1)
    spread = (jnp.arange(720, dtype=jnp.int32)[:, None] == home[None, :]).astype(BF)
    wtab = jnp.einsum("mol,lk->mok", wtab, spread, preferred_element_type=jnp.float32)
    wtab = wtab.astype(BF).reshape(2, PAIRS, OUT_ROWS, LATS * QPAD)

    field = jnp.pad(jnp.transpose(coarse_field, (1, 2, 0)), ((0, QPAD - ROWS), (0, 0), (0, 0)))
    field = field.reshape(LONS, QEACH, 180, CHAN)
    lon = lax.axis_index("lon")
    x, core = lon // 2, lon % 2
    pieces, held = [], []
    for dx, dc in ((2, 0), (2, 1), (1, 0), (3, 0), (1, 1), (3, 1), (0, 1), (0, 0)):
        part = pick(field, (x + dx) % 4 * 2 + (core + dc) % 2)
        if dx or dc:
            pairs = [(i, (i // 2 + dx) % 4 * 2 + (i + dc) % 2) for i in range(LONS)]
            part = lax.ppermute(part, "lon", pairs)
        pieces.append(part)
        held.append((x + 4 - dx) % 4 * 2 + (core + dc) % 2)

    a = jnp.arange(LATS * LONS * EACH, dtype=jnp.int32)
    slot = (a // (LONS * EACH)) * EACH + a % EACH
    column = (a // EACH) % LONS
    valid = (slot < OWN)[:, None]
    ids = (column * OWN + jnp.minimum(slot, OWN - 1))[:, None]
    points = jnp.stack(held)[:, None] * 180 + jnp.arange(180, dtype=jnp.int32)[None, :]
    points = points.reshape(1, LON_IN)
    cos_in, sin_in = lax.optimization_barrier(waves(ids, valid, points, LON_IN, LON_IN ** (-0.5)))
    field = jnp.concatenate(pieces, axis=1)
    parts = [
        jnp.einsum("np,qpc->nqc", t, field, preferred_element_type=jnp.float32).astype(BF)
        for t in (cos_in, sin_in)
    ]
    spectrum = jnp.concatenate(parts, axis=-1)
    spectrum = spectrum.reshape(LATS * LONS, EACH, QEACH, 2 * CHAN)
    spectrum, ftab = lax.optimization_barrier((spectrum, ftab))
    spectrum = swap(spectrum, ("lat", "lon")).reshape(LATS, LONS, EACH, QEACH, 2 * CHAN)
    spectrum = jnp.transpose(spectrum, (2, 0, 1, 3, 4)).reshape(EACH, LATS, QPAD, 2 * CHAN)
    spectrum = spectrum[:, :, :ROWS].reshape(EACH, 720, 2 * CHAN)

    coef = jnp.einsum("ajlq,jqn->ajln", ftab, spectrum, preferred_element_type=jnp.float32)
    coef = swap(coef.astype(BF), "lat").reshape(SLOTS, ROWS, 2 * CHAN)

    w = degree_mixing_weight
    turned = jnp.concatenate([-w[..., CHAN:], w[..., :CHAN]], axis=-1)
    both = jnp.concatenate([w, turned], axis=1)
    mixed = jnp.einsum("mlt,ltu->mlu", coef, both, preferred_element_type=jnp.float32)
    mixed = mixed.astype(BF)[:OWN].reshape(2, PAIRS, ROWS, 2 * CHAN)
    mixed = jnp.transpose(mixed, (1, 2, 0, 3)).reshape(PAIRS, ROWS, 4 * CHAN)
    mixed = jnp.pad(mixed, ((0, 0), (0, QPAD - ROWS), (0, 0)))
    mixed = lax.all_gather(mixed, "lat", axis=0)
    rows = synthesise(wtab, mixed)

    every = lax.all_gather(rows, "lon", axis=0, tiled=True)
    b = jnp.arange(LONS * PAIRS, dtype=jnp.int32)
    ids = b // PAIRS * OWN + b % PAIRS
    ids = jnp.stack([ids, ids + PAIRS])[:, :, None]
    t = jnp.arange(WIDE, dtype=jnp.int32)
    points = (lon * OUT_COLS + t)[None, None, :]
    cos_out, sin_out = waves(ids, t < OUT_COLS, points, LON_OUT, KEPT_ORDERS ** (-0.5))
    table = jnp.stack([cos_out, sin_out], axis=1).reshape(4, LONS * PAIRS, WIDE)
    table = lax.optimization_barrier(table)
    return to_longitudes(every, table)


def solution(mesh):
    in_specs = (
        P(None, "lat", "lon"),
        P("lon", "lat", None),
        P("lat", None, None),
        P("lon", None, "lat"),
    )
    out_specs = P(None, "lat", "lon")
    return jax.shard_map(local, mesh=mesh, in_specs=in_specs, out_specs=out_specs, check_vma=False)
```

```python
import functools
import math

import jax
import jax.numpy as jnp
from jax import lax
from jax.experimental import pallas as pl
from jax.experimental.pallas import tpu as pltpu
from jax.sharding import PartitionSpec as P

CHAN = 96
KEPT_ORDERS = 368
LON_IN = 1440
LON_OUT = 3600
LATS = 16
LONS = 8
OWN = 46
SLOTS = 48
EACH = 3
ROWS = 45
QPAD = 48
FAR = 32
PART = 12
HALF = 48
PAIRS = 23
OUT_ROWS = 64
OUT_COLS = 450
WIDE = 464
LANES = 128
STEP = 8
VMEM = 56 * 1024 * 1024
QEACH = 6
STEPS = ((2, 0), (2, 1), (1, 0), (3, 0), (1, 1), (3, 1), (0, 1), (0, 0))
BF = jnp.bfloat16


def waves(order_ids, turn, valid, points, modulus, factor):
    phases = (order_ids * points + turn * (modulus // 4)) % modulus
    angles = 2.0 * math.pi / modulus * phases.astype(jnp.float32)
    return (jnp.cos(angles) * jnp.where(valid, factor, 0.0)).astype(BF)


def swap(x, axis):
    return lax.all_to_all(x, axis, split_axis=0, concat_axis=0, tiled=True)


def synthesis_kernel(pairs, table, *refs):
    rows, lines = refs[-2:]
    p = pl.program_id(0)
    t = table[:, 0].reshape(2 * OUT_ROWS, LATS * QPAD)

    @pl.when(p == 0)
    def _():
        lines[...] = jnp.zeros_like(lines)

    m = jnp.concatenate([r[:, 0].reshape(-1, 4 * CHAN) for r in refs[:-2]], axis=0)
    both = jnp.dot(t, m, preferred_element_type=jnp.float32)
    lane = lax.broadcasted_iota(jnp.int32, (OUT_ROWS, 4 * CHAN), 1)
    one = jnp.where(lane < 2 * CHAN, both[:OUT_ROWS], both[OUT_ROWS:]).T
    for part in range(4):
        low = one[part * CHAN : part * CHAN + HALF]
        high = one[part * CHAN + HALF : (part + 1) * CHAN]
        side = jnp.concatenate([low, high], axis=1)
        lines[pl.ds(4 * p + part, HALF, stride=4 * PART), :] = side

    @pl.when(p == pairs - 1)
    def _():
        rows[...] = lines[...].reshape(rows.shape).astype(BF)


def synthesise(table, pieces):
    pairs = table.shape[1]
    return pl.pallas_call(
        functools.partial(synthesis_kernel, pairs),
        grid=(pairs,),
        in_specs=[pl.BlockSpec((2, 1, OUT_ROWS, LATS * QPAD), lambda p: (0, p, 0, 0))]
        + [pl.BlockSpec((v.shape[0], 1, QPAD, 4 * CHAN), lambda p: (0, p, 0, 0)) for v in pieces],
        out_specs=pl.BlockSpec((HALF, 4 * PART, LANES), lambda p: (0, 0, 0)),
        out_shape=jax.ShapeDtypeStruct((HALF, 4 * PART, LANES), BF),
        scratch_shapes=[pltpu.VMEM((HALF * 4 * PART, LANES), jnp.float32)],
        compiler_params=pltpu.CompilerParams(vmem_limit_bytes=VMEM),
        cost_estimate=pl.CostEstimate(
            flops=pairs * 2 * 128 * 768 * 384, bytes_accessed=pairs * 900000, transcendentals=0
        ),
    )(table, *pieces)


def output_kernel(table, *refs):
    out = refs[-1]

    def line(r, at):
        return r[at] if len(r.shape) == 3 else r[:, at].reshape(-1, LANES)

    for i in range(0, STEP, 2):
        both = [jnp.concatenate([line(r, i + k) for r in refs[:-1]], axis=0) for k in range(2)]
        both = jnp.concatenate(both, axis=1)
        made = jnp.dot(table[...], both, preferred_element_type=jnp.float32)
        made = made.astype(BF).T[:, :OUT_COLS]
        for k in range(2):
            for half in range(2):
                at = (2 * k + half) * OUT_ROWS
                out[half, i + k] = made[at : at + OUT_ROWS]


def to_longitudes(table, pieces):
    def spec(v):
        if v.ndim == 4:
            return pl.BlockSpec((v.shape[0], STEP, v.shape[2], LANES), lambda s: (0, s, 0, 0))
        return pl.BlockSpec((STEP, v.shape[1], LANES), lambda s: (s, 0, 0))

    out = pl.pallas_call(
        output_kernel,
        grid=(HALF // STEP,),
        in_specs=[pl.BlockSpec(table.shape, lambda s: (0, 0))]
        + [spec(v) for v in pieces],
        out_specs=pl.BlockSpec((2, STEP, OUT_ROWS, OUT_COLS), lambda s: (0, s, 0, 0)),
        out_shape=jax.ShapeDtypeStruct((2, HALF, OUT_ROWS, OUT_COLS), BF),
        compiler_params=pltpu.CompilerParams(vmem_limit_bytes=VMEM),
    )(table, *pieces)
    return out.reshape(CHAN, OUT_ROWS, OUT_COLS)


def pick(x, index):
    return lax.dynamic_index_in_dim(x, index, 0, keepdims=False)


def lat_shift(v, axis, d):
    if axis == "y":
        pairs = [(4 * y + z, 4 * ((y + d) % 4) + z) for y in range(4) for z in range(4)]
    else:
        pairs = [(4 * y + z, 4 * y + (z + d) % 4) for y in range(4) for z in range(4)]
    return lax.ppermute(v, "lat", pairs)


def gather_first(v, axis):
    half = v.shape[0] // 2
    up, down = lat_shift(v, axis, 1), lat_shift(v, axis, -1)
    far = [lat_shift(up[:half], axis, 1), lat_shift(down[half:], axis, -1)]
    return [jnp.stack([v, up]), jnp.stack([down, jnp.concatenate(far)])]


def gather_near(v, axis):
    up = [lat_shift(u, axis, 1) for u in v]
    down = [lat_shift(u, axis, -1) for u in v[::-1]][::-1]
    return v + up + down


def gather_far(v, axis):
    return v + [lat_shift(v[2], axis, 1), lat_shift(v[5], axis, -1)]


NEAR = (0, 1, 3, 2)


def sources(first, second):
    lat = lax.axis_index("lat")
    place = {"y": lat // 4, "z": lat % 4}
    found = []
    for g in NEAR:
        for e in NEAR:
            at = {second: (place[second] + 4 - g) % 4, first: (place[first] + 4 - e) % 4}
            found.append(at["y"] * 4 + at["z"])
    return jnp.stack(found)


def spread_table(table, order):
    row = jnp.arange(QPAD, dtype=jnp.int32)[None, :]
    home = jnp.where(row < ROWS, order[:, None] * ROWS + row, -1).reshape(-1)
    ones = (jnp.arange(720, dtype=jnp.int32)[:, None] == home[None, :]).astype(BF)
    return jnp.einsum("hmol,lk->hmok", table, ones, preferred_element_type=jnp.float32).astype(BF)


def lon_order(lines):
    lon = lax.axis_index("lon")
    half = FAR
    columns = [lon, (lon + 6) % 8, (lon + 2) % 8, (lon + 4) % 8, (lon + 4) % 8]
    ranges = [(0, lines), (0, lines), (0, lines), (0, half), (half, lines)]
    return columns + [c ^ 1 for c in columns], ranges * 2


def gather_lon(v):
    def along(u, d):
        return lax.ppermute(u, "lon", [(i, (i + 2 * d) % 8) for i in range(8)])

    def across(u):
        return lax.ppermute(u, "lon", [(i, i ^ 1) for i in range(8)])

    half = FAR
    right, left = along(v, 1), along(v, -1)
    far = [along(right[:, :half], 1), along(left[:, half:], -1)]
    pieces = [v, right, left] + far
    return pieces + [across(u) for u in pieces]


def local(coarse_field, forward_table, degree_mixing_weight, synthesis_weight_table):
    ftab = jnp.pad(forward_table, ((0, SLOTS - OWN), (0, 0), (0, 0)))
    ftab = ftab.reshape(LATS, EACH, ROWS, 720)
    ftab = swap(ftab, "lat")
    wtab = jnp.transpose(synthesis_weight_table, (0, 2, 1)).reshape(2, PAIRS, OUT_ROWS, 720)
    tables = [
        spread_table(wtab[:, :PART], sources("y", "z")),
        spread_table(wtab[:, PART:], sources("z", "y")),
    ]

    field = jnp.pad(jnp.transpose(coarse_field, (1, 2, 0)), ((0, QPAD - ROWS), (0, 0), (0, 0)))
    a = jnp.arange(LATS * LONS * EACH, dtype=jnp.int32)
    slot = (a // (LONS * EACH)) * EACH + a % EACH
    column = (a // EACH) % LONS
    valid = (slot < OWN)[:, None]
    ids = (column * OWN + jnp.minimum(slot, OWN - 1))[:, None]
    lon = lax.axis_index("lon")
    x, core = lon // 2, lon % 2
    held = [(x + 4 - dx) % 4 * 2 + (core + dc) % 2 for dx, dc in STEPS]
    points = jnp.stack(held)[:, None] * 180 + jnp.arange(180, dtype=jnp.int32)[None, :]
    points = points.reshape(1, LON_IN)
    phases = ids * points % LON_IN
    field = field.reshape(LONS, QEACH, 180, CHAN)
    phases, field = lax.optimization_barrier((phases, field))
    angles = 2.0 * math.pi / LON_IN * phases.astype(jnp.float32)
    factor = jnp.where(valid, LON_IN ** (-0.5), 0.0)
    waves_in = (jnp.cos(angles) * factor).astype(BF), (-jnp.sin(angles) * factor).astype(BF)
    waves_in = lax.optimization_barrier(waves_in)
    pieces = []
    for dx, dc in STEPS:
        part = pick(field, (x + dx) % 4 * 2 + (core + dc) % 2)
        if dx or dc:
            pairs = [(i, (i // 2 + dx) % 4 * 2 + (i + dc) % 2) for i in range(LONS)]
            part = lax.ppermute(part, "lon", pairs)
        pieces.append(part)
    field = jnp.concatenate(pieces, axis=1)
    parts = [
        jnp.einsum("np,qpc->nqc", t, field, preferred_element_type=jnp.float32).astype(BF)
        for t in waves_in
    ]
    spectrum = jnp.concatenate(parts, axis=-1)
    spectrum = spectrum.reshape(LATS * LONS, EACH, QEACH, 2 * CHAN)
    spectrum, ftab = lax.optimization_barrier((spectrum, ftab))
    spectrum = swap(spectrum, ("lat", "lon")).reshape(LATS, LONS, EACH, QEACH, 2 * CHAN)
    spectrum = jnp.transpose(spectrum, (2, 0, 1, 3, 4)).reshape(EACH, LATS, QPAD, 2 * CHAN)
    spectrum = spectrum[:, :, :ROWS].reshape(EACH, 720, 2 * CHAN)

    coef = jnp.einsum("ajlq,jqn->ajln", ftab, spectrum, preferred_element_type=jnp.float32)
    coef = swap(coef.astype(BF), "lat").reshape(SLOTS, ROWS, 2 * CHAN)

    ids, turns, real = [], [], []
    orders = [(0, column, 0, 4 * PART) for column in range(LONS)]
    orders += [(PART, c, a, b) for c, (a, b) in zip(*lon_order(4 * PART))]
    for pair, column, a, b in orders:
        line = jnp.arange(a, b, dtype=jnp.int32)
        at = pair + line // 4
        ids.append(column * OWN + at + line // 2 % 2 * PAIRS)
        turns.append(line % 2)
        real.append(at < PAIRS)
    ids, turns, real = (jnp.concatenate(v)[None, :] for v in (ids, turns, real))
    points = (lon * OUT_COLS + jnp.arange(WIDE, dtype=jnp.int32))[:, None]
    table = waves(ids, turns, real, points, LON_OUT, KEPT_ORDERS ** (-0.5))
    coef, table = lax.optimization_barrier((coef, table))

    w = degree_mixing_weight
    turned = jnp.concatenate([-w[..., CHAN:], w[..., :CHAN]], axis=-1)
    both = jnp.concatenate([w, turned], axis=1)
    mixed = jnp.einsum("mlt,ltu->mlu", coef, both, preferred_element_type=jnp.float32)
    mixed = mixed.astype(BF)[:OWN].reshape(2, PAIRS, ROWS, 2 * CHAN)
    mixed = jnp.transpose(mixed, (1, 2, 0, 3)).reshape(PAIRS, ROWS, 4 * CHAN)
    mixed = jnp.pad(mixed, ((0, 0), (0, QPAD - ROWS), (0, 0)))
    first, second = gather_first(mixed[:PART], "y"), gather_first(mixed[PART:], "z")
    first, second = lax.optimization_barrier((first, second))
    first, second = gather_near(first, "z"), gather_near(second, "y")
    first, second = gather_far(first, "z"), gather_far(second, "y")
    first, second = lax.optimization_barrier((first, second))
    early = lax.all_gather(synthesise(tables[0], first), "lon", axis=0)
    pieces = [early] + gather_lon(synthesise(tables[1], second))

    return to_longitudes(table, pieces)


def solution(mesh):
    in_specs = (
        P(None, "lat", "lon"),
        P("lon", "lat", None),
        P("lat", None, None),
        P("lon", None, "lat"),
    )
    out_specs = P(None, "lat", "lon")
    return jax.shard_map(local, mesh=mesh, in_specs=in_specs, out_specs=out_specs, check_vma=False)
```

```python
import math

import jax
import jax.numpy as jnp
from jax import lax
from jax.experimental import pallas as pl
from jax.experimental.pallas import tpu as pltpu
from jax.sharding import PartitionSpec as P

CHAN = 96
KEPT_ORDERS = 368
LON_IN = 1440
LON_OUT = 3600
LATS = 16
LONS = 8
OWN = 46
SLOTS = 48
EACH = 3
ROWS = 45
LINES = 2 * EACH
SPLIT = 64
HALF = 48
OUT_ROWS = 64
OUT_COLS = 450
WIDE = 464
LANES = 128
STEP = 8
VMEM = 56 * 1024 * 1024
BF = jnp.bfloat16


def waves(order_ids, turn, valid, points, modulus, factor):
    phases = (order_ids * points + turn * (modulus // 4)) % modulus
    angles = 2.0 * math.pi / modulus * phases.astype(jnp.float32)
    return (jnp.cos(angles) * jnp.where(valid, factor, 0.0)).astype(BF)


def swap(x, axis):
    return lax.all_to_all(x, axis, split_axis=0, concat_axis=0, tiled=True)


def share_kernel(waves_in, field, out):
    for q in range(0, field.shape[0], 2):
        some = [field[k] for k in range(q, min(q + 2, field.shape[0]))]
        some = jnp.concatenate([jnp.pad(v, ((0, 0), (0, LANES - CHAN))) for v in some], axis=1)
        made = jnp.dot(waves_in[...], some, preferred_element_type=jnp.float32).astype(BF)
        for k in range(some.shape[1] // LANES):
            one = made[:, k * LANES : k * LANES + CHAN].reshape(2, LONS, SLOTS, CHAN)
            for r in range(2):
                out[:, q + k, r * SLOTS : (r + 1) * SLOTS] = one[r]


def shares(waves_in, field):
    step = 9
    return pl.pallas_call(
        share_kernel,
        grid=(ROWS // step,),
        in_specs=[
            pl.BlockSpec(waves_in.shape, lambda s: (0, 0)),
            pl.BlockSpec((step, 180, CHAN), lambda s: (s, 0, 0)),
        ],
        out_specs=pl.BlockSpec((LONS, step, 2 * SLOTS, CHAN), lambda s: (0, s, 0, 0)),
        out_shape=jax.ShapeDtypeStruct((LONS, ROWS, 2 * SLOTS, CHAN), BF),
        compiler_params=pltpu.CompilerParams(vmem_limit_bytes=VMEM),
    )(waves_in, field)


def synthesis_kernel(mixed, table, rows, lines):
    made = []
    for k in range(EACH):
        t = table[:, k].reshape(LATS * OUT_ROWS, 720)
        made.append(jnp.dot(t, mixed[k], preferred_element_type=jnp.float32))
    for b in range(LATS):
        for k in range(EACH):
            one = made[k][b * OUT_ROWS : (b + 1) * OUT_ROWS].T
            for r in range(2):
                low, high = one[r * CHAN : r * CHAN + HALF], one[r * CHAN + HALF : (r + 1) * CHAN]
                side = jnp.concatenate([low, high], axis=1)
                lines[pl.ds(2 * k + r, HALF, stride=LINES), :] = side
        rows[b] = lines[...].astype(BF)


def synthesise(mixed, table):
    return pl.pallas_call(
        synthesis_kernel,
        out_shape=jax.ShapeDtypeStruct((LATS, HALF * LINES, LANES), BF),
        scratch_shapes=[pltpu.VMEM((HALF * LINES, LANES), jnp.float32)],
        compiler_params=pltpu.CompilerParams(vmem_limit_bytes=VMEM),
        cost_estimate=pl.CostEstimate(
            flops=2 * EACH * 1024 * 720 * 192, bytes_accessed=6000000, transcendentals=0
        ),
    )(mixed, table)


def joining_kernel(rows, out, rest, wide, lines):
    for a in range(LATS):
        wide[...] = rows[a].astype(jnp.float32)
        for k in range(LINES):
            one = wide[pl.ds(k, HALF, stride=LINES), :]
            lines[pl.ds(a * LINES + k, HALF, stride=LATS * LINES), :] = one
    made = lines[...].reshape(HALF, LATS * LINES, LANES).astype(BF)
    out[...] = made[:, :SPLIT]
    rest[...] = made[:, SPLIT:]


def join(rows):
    return pl.pallas_call(
        joining_kernel,
        out_shape=[
            jax.ShapeDtypeStruct((HALF, SPLIT, LANES), BF),
            jax.ShapeDtypeStruct((HALF, LATS * LINES - SPLIT, LANES), BF),
        ],
        scratch_shapes=[
            pltpu.VMEM((HALF * LINES, LANES), jnp.float32),
            pltpu.VMEM((HALF * LATS * LINES, LANES), jnp.float32),
        ],
        compiler_params=pltpu.CompilerParams(vmem_limit_bytes=VMEM),
    )(rows)


def output_kernel(table, *refs):
    out = refs[-1]

    def line(r, at):
        return r[at] if len(r.shape) == 3 else r[:, at].reshape(-1, LANES)

    for i in range(0, STEP, 2):
        both = [jnp.concatenate([line(r, i + k) for r in refs[:-1]], axis=0) for k in range(2)]
        both = jnp.concatenate(both, axis=1)
        made = jnp.dot(table[...], both, preferred_element_type=jnp.float32)
        made = made.astype(BF).T[:, :OUT_COLS]
        for k in range(2):
            for half in range(2):
                at = (2 * k + half) * OUT_ROWS
                out[half, i + k] = made[at : at + OUT_ROWS]


def to_longitudes(table, pieces):
    def spec(v):
        if v.ndim == 4:
            return pl.BlockSpec((v.shape[0], STEP, v.shape[2], LANES), lambda s: (0, s, 0, 0))
        return pl.BlockSpec((STEP, v.shape[1], LANES), lambda s: (s, 0, 0))

    out = pl.pallas_call(
        output_kernel,
        grid=(HALF // STEP,),
        in_specs=[pl.BlockSpec(table.shape, lambda s: (0, 0))] + [spec(v) for v in pieces],
        out_specs=pl.BlockSpec((2, STEP, OUT_ROWS, OUT_COLS), lambda s: (0, s, 0, 0)),
        out_shape=jax.ShapeDtypeStruct((2, HALF, OUT_ROWS, OUT_COLS), BF),
        compiler_params=pltpu.CompilerParams(vmem_limit_bytes=VMEM),
    )(table, *pieces)
    return out.reshape(CHAN, OUT_ROWS, OUT_COLS)


def lon_order():
    lon = lax.axis_index("lon")
    columns = [lon, (lon + 6) % 8, (lon + 2) % 8, (lon + 4) % 8]
    return columns + [c ^ 1 for c in columns]


def gather_lon(v):
    def along(u, d):
        return lax.ppermute(u, "lon", [(i, (i + 2 * d) % 8) for i in range(8)])

    def across(u):
        return lax.ppermute(u, "lon", [(i, i ^ 1) for i in range(8)])

    pieces = [v, along(v, 1), along(v, -1), along(v, 2)]
    return pieces + [across(u) for u in pieces]


def local(coarse_field, forward_table, degree_mixing_weight, synthesis_weight_table):
    ftab = jnp.pad(forward_table, ((0, SLOTS - OWN), (0, 0), (0, 0)))
    ftab = ftab.reshape(LATS, EACH, ROWS, 720)
    ftab, coarse_field = lax.optimization_barrier((ftab, coarse_field))
    ftab = swap(ftab, "lat")

    lon = lax.axis_index("lon")
    row = jnp.arange(2 * LONS * SLOTS, dtype=jnp.int32)[:, None]
    slot = row % SLOTS
    ids = row // SLOTS % LONS * OWN + jnp.minimum(slot, OWN - 1)
    points = (lon * 180 + jnp.arange(180, dtype=jnp.int32))[None, :]
    factor = LON_IN ** (-0.5)
    waves_in = waves(ids, row // (SLOTS * LONS), slot < OWN, points, LON_IN, factor)
    spectrum = shares(waves_in, jnp.transpose(coarse_field, (1, 2, 0)))

    wtab = jnp.transpose(synthesis_weight_table, (0, 2, 1))
    wtab = jnp.pad(wtab, ((0, SLOTS - OWN), (0, 0), (0, 0))).reshape(LATS, EACH, OUT_ROWS, 720)
    spectrum, ftab, wtab, lon = lax.optimization_barrier((spectrum, ftab, wtab, lon))
    spectrum = lax.psum_scatter(spectrum, "lon", scatter_dimension=0)
    wtab = swap(wtab, "lat")
    spectrum, wtab, lon = lax.optimization_barrier((spectrum, wtab, lon))
    spectrum = spectrum.reshape(ROWS, 2, LATS, EACH, CHAN)
    spectrum = jnp.transpose(spectrum, (2, 3, 0, 1, 4)).reshape(LATS, EACH, ROWS, 2 * CHAN)
    spectrum = swap(spectrum, "lat")
    spectrum = jnp.transpose(spectrum, (1, 0, 2, 3)).reshape(EACH, 720, 2 * CHAN)

    coef = jnp.einsum("ajlq,jqn->ajln", ftab, spectrum, preferred_element_type=jnp.float32)
    coef = swap(coef.astype(BF), "lat").reshape(SLOTS, ROWS, 2 * CHAN)

    ids, turns, real = [], [], []
    orders = [(column, 0, SPLIT) for column in range(LONS)]
    orders += [(column, SPLIT, 2 * SLOTS) for column in lon_order()]
    for column, first, last in orders:
        line = jnp.arange(first, last, dtype=jnp.int32)
        ids.append(column * OWN + jnp.minimum(line // 2, OWN - 1))
        turns.append(line % 2)
        real.append(line // 2 < OWN)
    ids, turns, real = (jnp.concatenate(v)[None, :] for v in (ids, turns, real))
    points = (lon * OUT_COLS + jnp.arange(WIDE, dtype=jnp.int32))[:, None]
    table = waves(ids, turns, real, points, LON_OUT, KEPT_ORDERS ** (-0.5))
    coef, table = lax.optimization_barrier((coef, table))

    w = degree_mixing_weight
    turned = jnp.concatenate([-w[..., CHAN:], w[..., :CHAN]], axis=-1)
    both = jnp.concatenate([w, turned], axis=1)
    mixed = jnp.einsum("mlt,ltu->mlu", coef, both, preferred_element_type=jnp.float32)
    mixed = swap(mixed.astype(BF).reshape(LATS, EACH, ROWS, 2 * CHAN), "lat")
    mixed = jnp.transpose(mixed, (1, 0, 2, 3)).reshape(EACH, 720, 2 * CHAN)
    rows, rest = join(swap(synthesise(mixed, wtab), "lat"))
    pieces = [lax.all_gather(rows, "lon", axis=0)] + gather_lon(rest)

    return to_longitudes(table, pieces)


def solution(mesh):
    in_specs = (
        P(None, "lat", "lon"),
        P("lon", "lat", None),
        P("lat", None, None),
        P("lon", None, "lat"),
    )
    out_specs = P(None, "lat", "lon")
    return jax.shard_map(local, mesh=mesh, in_specs=in_specs, out_specs=out_specs, check_vma=False)
```

```python
import math

import jax
import jax.numpy as jnp
from jax import lax
from jax.experimental import pallas as pl
from jax.experimental.pallas import tpu as pltpu
from jax.sharding import PartitionSpec as P

CHAN = 96
KEPT_ORDERS = 368
LON_IN = 1440
LON_OUT = 3600
LATS = 16
LONS = 8
OWN = 46
SLOTS = 48
EACH = 3
ROWS = 45
LINES = 2 * EACH
SPLIT = 64
HALF = 48
OUT_ROWS = 64
OUT_COLS = 450
WIDE = 464
LANES = 128
STEP = 8
MIB = 1024 * 1024
BF = jnp.bfloat16


def waves(order_ids, turn, valid, points, modulus, factor):
    phases = (order_ids * points + turn * (modulus // 4)) % modulus
    angles = 2.0 * math.pi / modulus * phases.astype(jnp.float32)
    return (jnp.cos(angles) * jnp.where(valid, factor, 0.0)).astype(BF)


def swap(x, axis):
    return lax.all_to_all(x, axis, split_axis=0, concat_axis=0, tiled=True)


def share_kernel(waves_in, field, out):
    for q in range(0, field.shape[0], 2):
        some = [field[k] for k in range(q, min(q + 2, field.shape[0]))]
        some = jnp.concatenate([jnp.pad(v, ((0, 0), (0, LANES - CHAN))) for v in some], axis=1)
        made = jnp.dot(waves_in[...], some, preferred_element_type=jnp.float32).astype(BF)
        for k in range(some.shape[1] // LANES):
            one = made[:, k * LANES : k * LANES + CHAN].reshape(2, LONS, SLOTS, CHAN)
            for r in range(2):
                out[:, q + k, r * SLOTS : (r + 1) * SLOTS] = one[r]


def shares(waves_in, field):
    step = 9
    return pl.pallas_call(
        share_kernel,
        grid=(ROWS // step,),
        in_specs=[
            pl.BlockSpec(waves_in.shape, lambda s: (0, 0)),
            pl.BlockSpec((step, 180, CHAN), lambda s: (s, 0, 0)),
        ],
        out_specs=pl.BlockSpec((LONS, step, 2 * SLOTS, CHAN), lambda s: (0, s, 0, 0)),
        out_shape=jax.ShapeDtypeStruct((LONS, ROWS, 2 * SLOTS, CHAN), BF),
        compiler_params=pltpu.CompilerParams(vmem_limit_bytes=16 * MIB),
    )(waves_in, field)


def synthesis_kernel(mixed, table, rows, lines):
    made = []
    for k in range(EACH):
        t = table[:, k].reshape(LATS * OUT_ROWS, 720)
        made.append(jnp.dot(t, mixed[k], preferred_element_type=jnp.float32))
    for b in range(LATS):
        for k in range(EACH):
            one = made[k][b * OUT_ROWS : (b + 1) * OUT_ROWS].T
            for r in range(2):
                low, high = one[r * CHAN : r * CHAN + HALF], one[r * CHAN + HALF : (r + 1) * CHAN]
                side = jnp.concatenate([low, high], axis=1)
                lines[pl.ds(2 * k + r, HALF, stride=LINES), :] = side
        rows[b] = lines[...].astype(BF)


def synthesise(mixed, table):
    return pl.pallas_call(
        synthesis_kernel,
        out_shape=jax.ShapeDtypeStruct((LATS, HALF * LINES, LANES), BF),
        scratch_shapes=[pltpu.VMEM((HALF * LINES, LANES), jnp.float32)],
        compiler_params=pltpu.CompilerParams(vmem_limit_bytes=20 * MIB),
        cost_estimate=pl.CostEstimate(
            flops=2 * EACH * 1024 * 720 * 192, bytes_accessed=6000000, transcendentals=0
        ),
    )(mixed, table)


def joining_kernel(rows, out, rest, wide, lines):
    for a in range(LATS):
        wide[...] = rows[a].astype(jnp.float32)
        for k in range(LINES):
            one = wide[pl.ds(k, HALF, stride=LINES), :]
            lines[pl.ds(a * LINES + k, HALF, stride=LATS * LINES), :] = one
    made = lines[...].reshape(HALF, LATS * LINES, LANES).astype(BF)
    out[...] = made[:, :SPLIT]
    rest[...] = made[:, SPLIT:]


def join(rows):
    return pl.pallas_call(
        joining_kernel,
        out_shape=[
            jax.ShapeDtypeStruct((HALF, SPLIT, LANES), BF),
            jax.ShapeDtypeStruct((HALF, LATS * LINES - SPLIT, LANES), BF),
        ],
        scratch_shapes=[
            pltpu.VMEM((HALF * LINES, LANES), jnp.float32),
            pltpu.VMEM((HALF * LATS * LINES, LANES), jnp.float32),
        ],
        compiler_params=pltpu.CompilerParams(vmem_limit_bytes=10 * MIB),
    )(rows)


def output_kernel(table, *refs):
    out = refs[-1]

    def line(r, at):
        return r[at] if len(r.shape) == 3 else r[:, at].reshape(-1, LANES)

    for i in range(0, STEP, 2):
        both = [jnp.concatenate([line(r, i + k) for r in refs[:-1]], axis=0) for k in range(2)]
        both = jnp.concatenate(both, axis=1)
        made = jnp.dot(table[...], both, preferred_element_type=jnp.float32)
        made = made.astype(BF).T[:, :OUT_COLS]
        for k in range(2):
            for half in range(2):
                at = (2 * k + half) * OUT_ROWS
                out[half, i + k] = made[at : at + OUT_ROWS]


def to_longitudes(table, pieces):
    def spec(v):
        if v.ndim == 4:
            return pl.BlockSpec((v.shape[0], STEP, v.shape[2], LANES), lambda s: (0, s, 0, 0))
        return pl.BlockSpec((STEP, v.shape[1], LANES), lambda s: (s, 0, 0))

    out = pl.pallas_call(
        output_kernel,
        grid=(HALF // STEP,),
        in_specs=[pl.BlockSpec(table.shape, lambda s: (0, 0))] + [spec(v) for v in pieces],
        out_specs=pl.BlockSpec((2, STEP, OUT_ROWS, OUT_COLS), lambda s: (0, s, 0, 0)),
        out_shape=jax.ShapeDtypeStruct((2, HALF, OUT_ROWS, OUT_COLS), BF),
        compiler_params=pltpu.CompilerParams(vmem_limit_bytes=56 * MIB),
    )(table, *pieces)
    return out.reshape(CHAN, OUT_ROWS, OUT_COLS)


def lon_order():
    lon = lax.axis_index("lon")
    columns = [lon, (lon + 6) % 8, (lon + 2) % 8, (lon + 4) % 8]
    return columns + [c ^ 1 for c in columns]


def gather_lon(v):
    def along(u, d):
        return lax.ppermute(u, "lon", [(i, (i + 2 * d) % 8) for i in range(8)])

    def across(u):
        return lax.ppermute(u, "lon", [(i, i ^ 1) for i in range(8)])

    pieces = [v, along(v, 1), along(v, -1), along(v, 2)]
    return pieces + [across(u) for u in pieces]


def local(coarse_field, forward_table, degree_mixing_weight, synthesis_weight_table):
    ftab = jnp.pad(forward_table, ((0, SLOTS - OWN), (0, 0), (0, 0)))
    ftab = ftab.reshape(LATS, EACH, ROWS, 720)
    ftab, coarse_field = lax.optimization_barrier((ftab, coarse_field))
    ftab = swap(ftab, "lat")

    lon = lax.axis_index("lon")
    row = jnp.arange(2 * LONS * SLOTS, dtype=jnp.int32)[:, None]
    slot = row % SLOTS
    ids = row // SLOTS % LONS * OWN + jnp.minimum(slot, OWN - 1)
    points = (lon * 180 + jnp.arange(180, dtype=jnp.int32))[None, :]
    factor = LON_IN ** (-0.5)
    waves_in = waves(ids, row // (SLOTS * LONS), slot < OWN, points, LON_IN, factor)
    spectrum = shares(waves_in, jnp.transpose(coarse_field, (1, 2, 0)))

    wtab = jnp.transpose(synthesis_weight_table, (0, 2, 1))
    wtab = jnp.pad(wtab, ((0, SLOTS - OWN), (0, 0), (0, 0))).reshape(LATS, EACH, OUT_ROWS, 720)
    spectrum, ftab, wtab, lon = lax.optimization_barrier((spectrum, ftab, wtab, lon))
    spectrum = lax.psum_scatter(spectrum, "lon", scatter_dimension=0)
    wtab = swap(wtab, "lat")
    spectrum, wtab, lon = lax.optimization_barrier((spectrum, wtab, lon))
    spectrum = spectrum.reshape(ROWS, 2, LATS, EACH, CHAN)
    spectrum = jnp.transpose(spectrum, (2, 3, 1, 0, 4))
    spectrum = swap(spectrum, "lat")
    spectrum = jnp.transpose(spectrum, (1, 0, 3, 2, 4)).reshape(EACH, 720, 2 * CHAN)

    coef = jnp.einsum("ajlq,jqn->ajln", ftab, spectrum, preferred_element_type=jnp.float32)
    coef = swap(coef.astype(BF), "lat").reshape(SLOTS, ROWS, 2 * CHAN)

    ids, turns, real = [], [], []
    orders = [(column, 0, SPLIT) for column in range(LONS)]
    orders += [(column, SPLIT, 2 * SLOTS) for column in lon_order()]
    for column, first, last in orders:
        line = jnp.arange(first, last, dtype=jnp.int32)
        ids.append(column * OWN + jnp.minimum(line // 2, OWN - 1))
        turns.append(line % 2)
        real.append(line // 2 < OWN)
    ids, turns, real = (jnp.concatenate(v)[None, :] for v in (ids, turns, real))
    points = (lon * OUT_COLS + jnp.arange(WIDE, dtype=jnp.int32))[:, None]
    table = waves(ids, turns, real, points, LON_OUT, KEPT_ORDERS ** (-0.5))
    coef, table = lax.optimization_barrier((coef, table))

    w = degree_mixing_weight
    turned = jnp.concatenate([-w[..., CHAN:], w[..., :CHAN]], axis=-1)
    both = jnp.concatenate([w, turned], axis=1)
    mixed = jnp.einsum("mlt,ltu->mlu", coef, both, preferred_element_type=jnp.float32)
    mixed = swap(mixed.astype(BF).reshape(LATS, EACH, ROWS, 2 * CHAN), "lat")
    mixed = jnp.transpose(mixed, (1, 0, 2, 3)).reshape(EACH, 720, 2 * CHAN)
    rows, rest = join(swap(synthesise(mixed, wtab), "lat"))
    pieces = [lax.all_gather(rows, "lon", axis=0)] + gather_lon(rest)

    return to_longitudes(table, pieces)


def solution(mesh):
    in_specs = (
        P(None, "lat", "lon"),
        P("lon", "lat", None),
        P("lat", None, None),
        P("lon", None, "lat"),
    )
    out_specs = P(None, "lat", "lon")
    return jax.shard_map(local, mesh=mesh, in_specs=in_specs, out_specs=out_specs, check_vma=False)
```

```python
import math

import jax
import jax.numpy as jnp
from jax import lax
from jax.experimental import pallas as pl
from jax.experimental.pallas import tpu as pltpu
from jax.sharding import PartitionSpec as P

CHAN = 96
KEPT_ORDERS = 368
LON_IN = 1440
LON_OUT = 3600
LATS = 16
LONS = 8
OWN = 46
SLOTS = 48
EACH = 3
ROWS = 45
LINES = 2 * EACH
SPLIT = 64
HALF = 48
OUT_ROWS = 64
OUT_COLS = 450
WIDE = 464
LANES = 128
STEP = 16
MIB = 1024 * 1024
BF = jnp.bfloat16


def waves(order_ids, turn, valid, points, modulus, factor):
    phases = (order_ids * points + turn * (modulus // 4)) % modulus
    angles = 2.0 * math.pi / modulus * phases.astype(jnp.float32)
    return (jnp.cos(angles) * jnp.where(valid, factor, 0.0)).astype(BF)


def swap(x, axis):
    return lax.all_to_all(x, axis, split_axis=0, concat_axis=0, tiled=True)


def share_kernel(waves_in, field, out):
    for q in range(0, field.shape[0], 2):
        some = [field[k] for k in range(q, min(q + 2, field.shape[0]))]
        some = jnp.concatenate([jnp.pad(v, ((0, 0), (0, LANES - CHAN))) for v in some], axis=1)
        made = jnp.dot(waves_in[...], some, preferred_element_type=jnp.float32).astype(BF)
        for k in range(some.shape[1] // LANES):
            one = made[:, k * LANES : k * LANES + CHAN].reshape(2, LONS, SLOTS, CHAN)
            for r in range(2):
                out[:, q + k, r * SLOTS : (r + 1) * SLOTS] = one[r]


def shares(waves_in, field):
    step = 9
    return pl.pallas_call(
        share_kernel,
        grid=(ROWS // step,),
        in_specs=[
            pl.BlockSpec(waves_in.shape, lambda s: (0, 0)),
            pl.BlockSpec((step, 180, CHAN), lambda s: (s, 0, 0)),
        ],
        out_specs=pl.BlockSpec((LONS, step, 2 * SLOTS, CHAN), lambda s: (0, s, 0, 0)),
        out_shape=jax.ShapeDtypeStruct((LONS, ROWS, 2 * SLOTS, CHAN), BF),
        compiler_params=pltpu.CompilerParams(vmem_limit_bytes=16 * MIB),
    )(waves_in, field)


def synthesis_kernel(mixed, table, rows, lines):
    made = []
    for k in range(EACH):
        t = table[:, k].reshape(LATS * OUT_ROWS, 720)
        made.append(jnp.dot(t, mixed[k], preferred_element_type=jnp.float32))
    for b in range(LATS):
        for k in range(EACH):
            one = made[k][b * OUT_ROWS : (b + 1) * OUT_ROWS].astype(BF).T.astype(jnp.float32)
            for r in range(2):
                low, high = one[r * CHAN : r * CHAN + HALF], one[r * CHAN + HALF : (r + 1) * CHAN]
                side = jnp.concatenate([low, high], axis=1)
                lines[pl.ds(2 * k + r, HALF, stride=LINES), :] = side
        rows[b] = lines[...].astype(BF)


def synthesise(mixed, table):
    return pl.pallas_call(
        synthesis_kernel,
        out_shape=jax.ShapeDtypeStruct((LATS, HALF * LINES, LANES), BF),
        scratch_shapes=[pltpu.VMEM((HALF * LINES, LANES), jnp.float32)],
        compiler_params=pltpu.CompilerParams(vmem_limit_bytes=20 * MIB),
        cost_estimate=pl.CostEstimate(
            flops=2 * EACH * 1024 * 720 * 192, bytes_accessed=6000000, transcendentals=0
        ),
    )(mixed, table)


def joining_kernel(rows, out, rest, wide, lines):
    for a in range(LATS):
        wide[...] = rows[a].astype(jnp.float32)
        for k in range(LINES):
            one = wide[pl.ds(k, HALF, stride=LINES), :]
            lines[pl.ds(a * LINES + k, HALF, stride=LATS * LINES), :] = one
    made = lines[...].reshape(HALF, LATS * LINES, LANES).astype(BF)
    out[...] = made[:, :SPLIT]
    rest[...] = made[:, SPLIT:]


def join(rows):
    return pl.pallas_call(
        joining_kernel,
        out_shape=[
            jax.ShapeDtypeStruct((HALF, SPLIT, LANES), BF),
            jax.ShapeDtypeStruct((HALF, LATS * LINES - SPLIT, LANES), BF),
        ],
        scratch_shapes=[
            pltpu.VMEM((HALF * LINES, LANES), jnp.float32),
            pltpu.VMEM((HALF * LATS * LINES, LANES), jnp.float32),
        ],
        compiler_params=pltpu.CompilerParams(vmem_limit_bytes=10 * MIB),
    )(rows)


def output_kernel(table, *refs):
    out = refs[-1]

    def line(r, at):
        return r[at] if len(r.shape) == 3 else r[:, at].reshape(-1, LANES)

    for i in range(0, STEP, 2):
        both = [jnp.concatenate([line(r, i + k) for r in refs[:-1]], axis=0) for k in range(2)]
        both = jnp.concatenate(both, axis=1)
        made = jnp.dot(table[...], both, preferred_element_type=jnp.float32)
        made = made.astype(BF).T[:, :OUT_COLS]
        for k in range(2):
            for half in range(2):
                at = (2 * k + half) * OUT_ROWS
                out[half, i + k] = made[at : at + OUT_ROWS]


def to_longitudes(table, pieces):
    def spec(v):
        if v.ndim == 4:
            return pl.BlockSpec((v.shape[0], STEP, v.shape[2], LANES), lambda s: (0, s, 0, 0))
        return pl.BlockSpec((STEP, v.shape[1], LANES), lambda s: (s, 0, 0))

    out = pl.pallas_call(
        output_kernel,
        grid=(HALF // STEP,),
        in_specs=[pl.BlockSpec(table.shape, lambda s: (0, 0))] + [spec(v) for v in pieces],
        out_specs=pl.BlockSpec((2, STEP, OUT_ROWS, OUT_COLS), lambda s: (0, s, 0, 0)),
        out_shape=jax.ShapeDtypeStruct((2, HALF, OUT_ROWS, OUT_COLS), BF),
        compiler_params=pltpu.CompilerParams(vmem_limit_bytes=56 * MIB),
    )(table, *pieces)
    return out.reshape(CHAN, OUT_ROWS, OUT_COLS)


def lon_order(first, last):
    lon = lax.axis_index("lon")
    columns = [lon, (lon + 6) % 8, (lon + 2) % 8, (lon + 4) % 8, (lon + 4) % 8]
    half = (first + last) // 2
    ranges = [(first, last), (first, last), (first, last), (first, half), (half, last)]
    return [(c, *r) for c, r in zip(columns + [c ^ 1 for c in columns], ranges * 2)]


def gather_lon(v):
    def along(u, d):
        return lax.ppermute(u, "lon", [(i, (i + 2 * d) % 8) for i in range(8)])

    def across(u):
        return lax.ppermute(u, "lon", [(i, i ^ 1) for i in range(8)])

    half = v.shape[1] // 2
    right, left = along(v, 1), along(v, -1)
    far = [along(right[:, :half], 1), along(left[:, half:], -1)]
    pieces = [v, right, left] + far
    return pieces + [across(u) for u in pieces]


def local(coarse_field, forward_table, degree_mixing_weight, synthesis_weight_table):
    ftab = jnp.pad(forward_table, ((0, SLOTS - OWN), (0, 0), (0, 0)))
    ftab = ftab.reshape(LATS, EACH * ROWS, 720)
    ftab, coarse_field = lax.optimization_barrier((ftab, coarse_field))
    ftab = swap(ftab, "lat")

    lon = lax.axis_index("lon")
    row = jnp.arange(2 * LONS * SLOTS, dtype=jnp.int32)[:, None]
    slot = row % SLOTS
    ids = row // SLOTS % LONS * OWN + jnp.minimum(slot, OWN - 1)
    points = (lon * 180 + jnp.arange(180, dtype=jnp.int32))[None, :]
    factor = LON_IN ** (-0.5)
    waves_in = waves(ids, row // (SLOTS * LONS), slot < OWN, points, LON_IN, factor)
    spectrum = shares(waves_in, jnp.transpose(coarse_field, (1, 2, 0)))

    wtab = jnp.transpose(synthesis_weight_table, (0, 2, 1))
    wtab = jnp.pad(wtab, ((0, SLOTS - OWN), (0, 0), (0, 0))).reshape(LATS, EACH, OUT_ROWS, 720)
    spectrum, ftab, wtab, lon = lax.optimization_barrier((spectrum, ftab, wtab, lon))
    spectrum = lax.psum_scatter(spectrum, "lon", scatter_dimension=0)
    wtab = swap(wtab, "lat")
    ftab = ftab.reshape(LATS, EACH, ROWS, 720)
    spectrum = spectrum.reshape(ROWS, 2, LATS, EACH, CHAN)
    spectrum = jnp.transpose(spectrum, (2, 3, 1, 0, 4))
    spectrum, wtab, lon = lax.optimization_barrier((spectrum, wtab, lon))
    spectrum = swap(spectrum, "lat")
    spectrum = jnp.transpose(spectrum, (1, 0, 3, 2, 4)).reshape(EACH, 720, 2 * CHAN)

    coef = jnp.einsum("ajlq,jqn->ajln", ftab, spectrum, preferred_element_type=jnp.float32)
    coef = swap(coef.astype(BF), "lat").reshape(SLOTS, ROWS, 2 * CHAN)

    ids, turns, real = [], [], []
    orders = [(column, 0, SPLIT) for column in range(LONS)]
    orders += lon_order(SPLIT, 2 * SLOTS)
    for column, first, last in orders:
        line = jnp.arange(first, last, dtype=jnp.int32)
        ids.append(column * OWN + jnp.minimum(line // 2, OWN - 1))
        turns.append(line % 2)
        real.append(line // 2 < OWN)
    ids, turns, real = (jnp.concatenate(v)[None, :] for v in (ids, turns, real))
    points = (lon * OUT_COLS + jnp.arange(WIDE, dtype=jnp.int32))[:, None]
    table = waves(ids, turns, real, points, LON_OUT, KEPT_ORDERS ** (-0.5))
    coef, table = lax.optimization_barrier((coef, table))

    w = degree_mixing_weight
    turned = jnp.concatenate([-w[..., CHAN:], w[..., :CHAN]], axis=-1)
    both = jnp.concatenate([w, turned], axis=1)
    mixed = jnp.einsum("mlt,ltu->mlu", coef, both, preferred_element_type=jnp.float32)
    mixed = swap(mixed.astype(BF).reshape(LATS, EACH, ROWS, 2 * CHAN), "lat")
    mixed = jnp.transpose(mixed, (1, 0, 2, 3)).reshape(EACH, 720, 2 * CHAN)
    rows, rest = join(swap(synthesise(mixed, wtab), "lat"))
    pieces = [lax.all_gather(rows, "lon", axis=0)] + gather_lon(rest)

    return to_longitudes(table, pieces)


def solution(mesh):
    in_specs = (
        P(None, "lat", "lon"),
        P("lon", "lat", None),
        P("lat", None, None),
        P("lon", None, "lat"),
    )
    out_specs = P(None, "lat", "lon")
    return jax.shard_map(local, mesh=mesh, in_specs=in_specs, out_specs=out_specs, check_vma=False)
```

```python
import math

import jax
import jax.numpy as jnp
from jax import lax
from jax.experimental import pallas as pl
from jax.experimental.pallas import tpu as pltpu
from jax.sharding import PartitionSpec as P

CHAN = 96
KEPT_ORDERS = 368
LON_IN = 1440
LON_OUT = 3600
LATS = 16
LONS = 8
OWN = 46
SLOTS = 48
EACH = 3
ROWS = 45
LINES = 2 * EACH
SPLIT = 64
HALF = 48
OUT_ROWS = 64
OUT_COLS = 450
WIDE = 464
LANES = 128
PAIRED, EIGHTS, PACKED = 960, 1056, 1088
STEP = 16
MIB = 1024 * 1024
BF = jnp.bfloat16


def waves(order_ids, turn, valid, points, modulus, factor):
    phases = (order_ids * points + turn * (modulus // 4)) % modulus
    angles = 2.0 * math.pi / modulus * phases.astype(jnp.float32)
    return (jnp.cos(angles) * jnp.where(valid, factor, 0.0)).astype(BF)


def swap(x, axis):
    return lax.all_to_all(x, axis, split_axis=0, concat_axis=0, tiled=True)


def share_kernel(waves_in, field, out):
    for q in range(0, field.shape[0], 2):
        some = [field[k] for k in range(q, min(q + 2, field.shape[0]))]
        some = jnp.concatenate([jnp.pad(v, ((0, 0), (0, LANES - CHAN))) for v in some], axis=1)
        made = jnp.dot(waves_in[...], some, preferred_element_type=jnp.float32).astype(BF)
        for k in range(some.shape[1] // LANES):
            one = made[:, k * LANES : k * LANES + CHAN].reshape(2, LONS, SLOTS, CHAN)
            for r in range(2):
                out[:, q + k, r * SLOTS : (r + 1) * SLOTS] = one[r]


def shares(waves_in, field):
    step = 9
    return pl.pallas_call(
        share_kernel,
        grid=(ROWS // step,),
        in_specs=[
            pl.BlockSpec(waves_in.shape, lambda s: (0, 0)),
            pl.BlockSpec((step, 180, CHAN), lambda s: (s, 0, 0)),
        ],
        out_specs=pl.BlockSpec((LONS, step, 2 * SLOTS, CHAN), lambda s: (0, s, 0, 0)),
        out_shape=jax.ShapeDtypeStruct((LONS, ROWS, 2 * SLOTS, CHAN), BF),
        compiler_params=pltpu.CompilerParams(vmem_limit_bytes=16 * MIB),
    )(waves_in, field)


def packing_kernel(*refs):
    out = refs[-1]
    ends = []
    for k, table in enumerate(refs[:-1]):
        for t in range(5):
            at = (5 * k + t) * OUT_ROWS
            out[0, at : at + OUT_ROWS] = table[0, :, t * LANES : (t + 1) * LANES]
        rest = table[0, :, 640:704]
        at = PAIRED + k * 32
        out[0, at : at + 32] = jnp.concatenate([rest[:32], rest[32:]], axis=1)
        rest = table[0, :, 704:].astype(jnp.float32)
        ends.append(jnp.concatenate([rest[8 * g : 8 * g + 8] for g in range(8)], axis=1))
    ends.append(jnp.zeros((8, LANES), jnp.float32))
    out[0, EIGHTS:] = jnp.concatenate(ends, axis=0).astype(BF)

    @pl.when(pl.program_id(0) == LATS - 1)
    def _():
        for k in range(OWN - (LATS - 1) * EACH, EACH):
            out[0, 5 * k * OUT_ROWS : 5 * (k + 1) * OUT_ROWS] = jnp.zeros((5 * OUT_ROWS, LANES), BF)
            out[0, PAIRED + k * 32 : PAIRED + (k + 1) * 32] = jnp.zeros((32, LANES), BF)
        there = lax.broadcasted_iota(jnp.int32, (32, LANES), 0) < 8 * (OWN - (LATS - 1) * EACH)
        last = jnp.where(there, jnp.concatenate(ends, axis=0), 0.0)
        out[0, EIGHTS:] = last.astype(BF)


def pack(table):
    def spec(k):
        return pl.BlockSpec(
            (1, OUT_ROWS, 720), lambda a: (jnp.minimum(a * EACH + k, OWN - 1), 0, 0)
        )

    return pl.pallas_call(
        packing_kernel,
        grid=(LATS,),
        in_specs=[spec(k) for k in range(EACH)],
        out_specs=pl.BlockSpec((1, PACKED, LANES), lambda a: (a, 0, 0)),
        out_shape=jax.ShapeDtypeStruct((LATS, PACKED, LANES), BF),
        compiler_params=pltpu.CompilerParams(vmem_limit_bytes=10 * MIB),
    )(*[table] * EACH)


def unpack(table, k):
    parts = []
    for t in range(5):
        at = (5 * k + t) * OUT_ROWS
        parts.append(table[:, at : at + OUT_ROWS].reshape(LATS * OUT_ROWS, LANES))
    pairs = table[:, PAIRED + k * 32 : PAIRED + (k + 1) * 32]
    pairs = jnp.concatenate([pairs[:, :, :64], pairs[:, :, 64:]], axis=1)
    ends = table[:, EIGHTS:].astype(jnp.float32)[:, 8 * k : 8 * k + 8]
    ends = jnp.concatenate([ends[:, :, 16 * g : 16 * g + 16] for g in range(8)], axis=1)
    ends = ends.reshape(LATS * OUT_ROWS, 16).astype(BF)
    return jnp.concatenate(parts + [pairs.reshape(LATS * OUT_ROWS, 64), ends], axis=1)


def synthesis_kernel(mixed, table, rows, lines):
    made = []
    for k in range(EACH):
        made.append(jnp.dot(unpack(table, k), mixed[k], preferred_element_type=jnp.float32))
    for b in range(LATS):
        for k in range(EACH):
            one = made[k][b * OUT_ROWS : (b + 1) * OUT_ROWS].astype(BF).T.astype(jnp.float32)
            for r in range(2):
                low, high = one[r * CHAN : r * CHAN + HALF], one[r * CHAN + HALF : (r + 1) * CHAN]
                side = jnp.concatenate([low, high], axis=1)
                lines[pl.ds(2 * k + r, HALF, stride=LINES), :] = side
        rows[b] = lines[...].astype(BF)


def synthesise(mixed, table):
    return pl.pallas_call(
        synthesis_kernel,
        out_shape=jax.ShapeDtypeStruct((LATS, HALF * LINES, LANES), BF),
        scratch_shapes=[pltpu.VMEM((HALF * LINES, LANES), jnp.float32)],
        compiler_params=pltpu.CompilerParams(vmem_limit_bytes=32 * MIB),
        cost_estimate=pl.CostEstimate(
            flops=2 * EACH * 1024 * 720 * 192, bytes_accessed=6000000, transcendentals=0
        ),
    )(mixed, table)


def joining_kernel(rows, out, rest, wide, lines):
    for a in range(LATS):
        wide[...] = rows[a].astype(jnp.float32)
        for k in range(LINES):
            one = wide[pl.ds(k, HALF, stride=LINES), :]
            lines[pl.ds(a * LINES + k, HALF, stride=LATS * LINES), :] = one
    made = lines[...].reshape(HALF, LATS * LINES, LANES).astype(BF)
    out[...] = made[:, :SPLIT]
    rest[...] = made[:, SPLIT:]


def join(rows):
    return pl.pallas_call(
        joining_kernel,
        out_shape=[
            jax.ShapeDtypeStruct((HALF, SPLIT, LANES), BF),
            jax.ShapeDtypeStruct((HALF, LATS * LINES - SPLIT, LANES), BF),
        ],
        scratch_shapes=[
            pltpu.VMEM((HALF * LINES, LANES), jnp.float32),
            pltpu.VMEM((HALF * LATS * LINES, LANES), jnp.float32),
        ],
        compiler_params=pltpu.CompilerParams(vmem_limit_bytes=10 * MIB),
    )(rows)


def output_kernel(table, *refs):
    out = refs[-1]

    def line(r, at):
        return r[at] if len(r.shape) == 3 else r[:, at].reshape(-1, LANES)

    for i in range(0, STEP, 2):
        both = [jnp.concatenate([line(r, i + k) for r in refs[:-1]], axis=0) for k in range(2)]
        both = jnp.concatenate(both, axis=1)
        made = jnp.dot(table[...], both, preferred_element_type=jnp.float32)
        made = made.astype(BF).T[:, :OUT_COLS]
        for k in range(2):
            for half in range(2):
                at = (2 * k + half) * OUT_ROWS
                out[half, i + k] = made[at : at + OUT_ROWS]


def to_longitudes(table, pieces):
    def spec(v):
        if v.ndim == 4:
            return pl.BlockSpec((v.shape[0], STEP, v.shape[2], LANES), lambda s: (0, s, 0, 0))
        return pl.BlockSpec((STEP, v.shape[1], LANES), lambda s: (s, 0, 0))

    out = pl.pallas_call(
        output_kernel,
        grid=(HALF // STEP,),
        in_specs=[pl.BlockSpec(table.shape, lambda s: (0, 0))] + [spec(v) for v in pieces],
        out_specs=pl.BlockSpec((2, STEP, OUT_ROWS, OUT_COLS), lambda s: (0, s, 0, 0)),
        out_shape=jax.ShapeDtypeStruct((2, HALF, OUT_ROWS, OUT_COLS), BF),
        compiler_params=pltpu.CompilerParams(vmem_limit_bytes=56 * MIB),
    )(table, *pieces)
    return out.reshape(CHAN, OUT_ROWS, OUT_COLS)


def lon_order(first, last):
    lon = lax.axis_index("lon")
    columns = [lon, (lon + 6) % 8, (lon + 2) % 8, (lon + 4) % 8, (lon + 4) % 8]
    half = (first + last) // 2
    ranges = [(first, last), (first, last), (first, last), (first, half), (half, last)]
    return [(c, *r) for c, r in zip(columns + [c ^ 1 for c in columns], ranges * 2)]


def gather_lon(v):
    def along(u, d):
        return lax.ppermute(u, "lon", [(i, (i + 2 * d) % 8) for i in range(8)])

    def across(u):
        return lax.ppermute(u, "lon", [(i, i ^ 1) for i in range(8)])

    half = v.shape[1] // 2
    right, left = along(v, 1), along(v, -1)
    far = [along(right[:, :half], 1), along(left[:, half:], -1)]
    pieces = [v, right, left] + far
    return pieces + [across(u) for u in pieces]


def local(coarse_field, forward_table, degree_mixing_weight, synthesis_weight_table):
    ftab = jnp.pad(forward_table, ((0, SLOTS - OWN), (0, 0), (0, 0)))
    ftab = ftab.reshape(LATS, EACH * ROWS, 720)
    ftab, coarse_field = lax.optimization_barrier((ftab, coarse_field))
    ftab = swap(ftab, "lat")

    lon = lax.axis_index("lon")
    row = jnp.arange(2 * LONS * SLOTS, dtype=jnp.int32)[:, None]
    slot = row % SLOTS
    ids = row // SLOTS % LONS * OWN + jnp.minimum(slot, OWN - 1)
    points = (lon * 180 + jnp.arange(180, dtype=jnp.int32))[None, :]
    factor = LON_IN ** (-0.5)
    waves_in = waves(ids, row // (SLOTS * LONS), slot < OWN, points, LON_IN, factor)
    spectrum = shares(waves_in, jnp.transpose(coarse_field, (1, 2, 0)))

    wtab = pack(jnp.transpose(synthesis_weight_table, (0, 2, 1)))
    spectrum, ftab, wtab, lon = lax.optimization_barrier((spectrum, ftab, wtab, lon))
    spectrum = lax.psum_scatter(spectrum, "lon", scatter_dimension=0)
    wtab = swap(wtab, "lat")
    ftab = ftab.reshape(LATS, EACH, ROWS, 720)
    spectrum = spectrum.reshape(ROWS, 2, LATS, EACH, CHAN)
    spectrum = jnp.transpose(spectrum, (2, 3, 1, 0, 4))
    spectrum, wtab, lon = lax.optimization_barrier((spectrum, wtab, lon))
    spectrum = swap(spectrum, "lat")
    spectrum = jnp.transpose(spectrum, (1, 0, 3, 2, 4)).reshape(EACH, 720, 2 * CHAN)

    coef = jnp.einsum("ajlq,jqn->ajln", ftab, spectrum, preferred_element_type=jnp.float32)
    coef = swap(coef.astype(BF), "lat").reshape(SLOTS, ROWS, 2 * CHAN)

    ids, turns, real = [], [], []
    orders = [(column, 0, SPLIT) for column in range(LONS)]
    orders += lon_order(SPLIT, 2 * SLOTS)
    for column, first, last in orders:
        line = jnp.arange(first, last, dtype=jnp.int32)
        ids.append(column * OWN + jnp.minimum(line // 2, OWN - 1))
        turns.append(line % 2)
        real.append(line // 2 < OWN)
    ids, turns, real = (jnp.concatenate(v)[None, :] for v in (ids, turns, real))
    points = (lon * OUT_COLS + jnp.arange(WIDE, dtype=jnp.int32))[:, None]
    table = waves(ids, turns, real, points, LON_OUT, KEPT_ORDERS ** (-0.5))
    coef, table = lax.optimization_barrier((coef, table))

    w = degree_mixing_weight
    turned = jnp.concatenate([-w[..., CHAN:], w[..., :CHAN]], axis=-1)
    both = jnp.concatenate([w, turned], axis=1)
    mixed = jnp.einsum("mlt,ltu->mlu", coef, both, preferred_element_type=jnp.float32)
    mixed = swap(mixed.astype(BF).reshape(LATS, EACH, ROWS, 2 * CHAN), "lat")
    mixed = jnp.transpose(mixed, (1, 0, 2, 3)).reshape(EACH, 720, 2 * CHAN)
    rows, rest = join(swap(synthesise(mixed, wtab), "lat"))
    pieces = [lax.all_gather(rows, "lon", axis=0)] + gather_lon(rest)

    return to_longitudes(table, pieces)


def solution(mesh):
    in_specs = (
        P(None, "lat", "lon"),
        P("lon", "lat", None),
        P("lat", None, None),
        P("lon", None, "lat"),
    )
    out_specs = P(None, "lat", "lon")
    return jax.shard_map(local, mesh=mesh, in_specs=in_specs, out_specs=out_specs, check_vma=False)
```

```python
import math

import jax
import jax.numpy as jnp
from jax import lax
from jax.experimental import pallas as pl
from jax.experimental.pallas import tpu as pltpu
from jax.sharding import PartitionSpec as P

CHAN = 96
KEPT_ORDERS = 368
LON_IN = 1440
LON_OUT = 3600
LATS = 16
LONS = 8
OWN = 46
SLOTS = 48
EACH = 3
ROWS = 45
LINES = 2 * EACH
SPLIT = 64
HALF = 48
OUT_ROWS = 64
OUT_COLS = 450
WIDE = 464
LANES = 128
PAIRED, EIGHTS, PACKED = 960, 1056, 1088
STEP = 16
MIB = 1024 * 1024
BF = jnp.bfloat16


def waves(order_ids, turn, valid, points, modulus, factor):
    phases = (order_ids * points + turn * (modulus // 4)) % modulus
    angles = 2.0 * math.pi / modulus * phases.astype(jnp.float32)
    return (jnp.cos(angles) * jnp.where(valid, factor, 0.0)).astype(BF)


def swap(x, axis):
    return lax.all_to_all(x, axis, split_axis=0, concat_axis=0, tiled=True)


def share_kernel(waves_in, field, out):
    for q in range(0, field.shape[0], 2):
        some = [field[k] for k in range(q, min(q + 2, field.shape[0]))]
        some = jnp.concatenate([jnp.pad(v, ((0, 0), (0, LANES - CHAN))) for v in some], axis=1)
        made = jnp.dot(waves_in[...], some, preferred_element_type=jnp.float32).astype(BF)
        for k in range(some.shape[1] // LANES):
            one = made[:, k * LANES : k * LANES + CHAN].reshape(2, LONS, SLOTS, CHAN)
            for r in range(2):
                out[:, q + k, r * SLOTS : (r + 1) * SLOTS] = one[r]


def shares(waves_in, field):
    step = 9
    return pl.pallas_call(
        share_kernel,
        grid=(ROWS // step,),
        in_specs=[
            pl.BlockSpec(waves_in.shape, lambda s: (0, 0)),
            pl.BlockSpec((step, 180, CHAN), lambda s: (s, 0, 0)),
        ],
        out_specs=pl.BlockSpec((LONS, step, 2 * SLOTS, CHAN), lambda s: (0, s, 0, 0)),
        out_shape=jax.ShapeDtypeStruct((LONS, ROWS, 2 * SLOTS, CHAN), BF),
        compiler_params=pltpu.CompilerParams(vmem_limit_bytes=16 * MIB),
    )(waves_in, field)


def packing_kernel(*refs):
    out = refs[-1]
    ends = []
    for k, table in enumerate(refs[:-1]):
        for t in range(5):
            at = (5 * k + t) * OUT_ROWS
            out[0, at : at + OUT_ROWS] = table[0, :, t * LANES : (t + 1) * LANES]
        rest = table[0, :, 640:704]
        at = PAIRED + k * 32
        out[0, at : at + 32] = jnp.concatenate([rest[:32], rest[32:]], axis=1)
        rest = table[0, :, 704:].astype(jnp.float32)
        ends.append(jnp.concatenate([rest[8 * g : 8 * g + 8] for g in range(8)], axis=1))
    ends.append(jnp.zeros((8, LANES), jnp.float32))
    out[0, EIGHTS:] = jnp.concatenate(ends, axis=0).astype(BF)

    @pl.when(pl.program_id(0) == LATS - 1)
    def _():
        for k in range(OWN - (LATS - 1) * EACH, EACH):
            out[0, 5 * k * OUT_ROWS : 5 * (k + 1) * OUT_ROWS] = jnp.zeros((5 * OUT_ROWS, LANES), BF)
            out[0, PAIRED + k * 32 : PAIRED + (k + 1) * 32] = jnp.zeros((32, LANES), BF)
        there = lax.broadcasted_iota(jnp.int32, (32, LANES), 0) < 8 * (OWN - (LATS - 1) * EACH)
        last = jnp.where(there, jnp.concatenate(ends, axis=0), 0.0)
        out[0, EIGHTS:] = last.astype(BF)


def pack(table):
    def spec(k):
        return pl.BlockSpec(
            (1, OUT_ROWS, 720), lambda a: (jnp.minimum(a * EACH + k, OWN - 1), 0, 0)
        )

    return pl.pallas_call(
        packing_kernel,
        grid=(LATS,),
        in_specs=[spec(k) for k in range(EACH)],
        out_specs=pl.BlockSpec((1, PACKED, LANES), lambda a: (a, 0, 0)),
        out_shape=jax.ShapeDtypeStruct((LATS, PACKED, LANES), BF),
        compiler_params=pltpu.CompilerParams(vmem_limit_bytes=10 * MIB),
    )(*[table] * EACH)


def unpack(table, k):
    parts = []
    for t in range(5):
        at = (5 * k + t) * OUT_ROWS
        parts.append(table[:, at : at + OUT_ROWS].reshape(LATS * OUT_ROWS, LANES))
    pairs = table[:, PAIRED + k * 32 : PAIRED + (k + 1) * 32]
    pairs = jnp.concatenate([pairs[:, :, :64], pairs[:, :, 64:]], axis=1)
    ends = table[:, EIGHTS:].astype(jnp.float32)[:, 8 * k : 8 * k + 8]
    ends = jnp.concatenate([ends[:, :, 16 * g : 16 * g + 16] for g in range(8)], axis=1)
    ends = ends.reshape(LATS * OUT_ROWS, 16).astype(BF)
    return jnp.concatenate(parts + [pairs.reshape(LATS * OUT_ROWS, 64), ends], axis=1)


def synthesis_kernel(mixed, table, rows, lines):
    made = []
    for k in range(EACH):
        made.append(jnp.dot(unpack(table, k), mixed[k], preferred_element_type=jnp.float32))
    for b in range(LATS):
        for k in range(EACH):
            one = made[k][b * OUT_ROWS : (b + 1) * OUT_ROWS].astype(BF).T.astype(jnp.float32)
            for r in range(2):
                low, high = one[r * CHAN : r * CHAN + HALF], one[r * CHAN + HALF : (r + 1) * CHAN]
                side = jnp.concatenate([low, high], axis=1)
                lines[pl.ds(2 * k + r, HALF, stride=LINES), :] = side
        rows[b] = lines[...].astype(BF)


def synthesise(mixed, table):
    return pl.pallas_call(
        synthesis_kernel,
        out_shape=jax.ShapeDtypeStruct((LATS, HALF * LINES, LANES), BF),
        scratch_shapes=[pltpu.VMEM((HALF * LINES, LANES), jnp.float32)],
        compiler_params=pltpu.CompilerParams(vmem_limit_bytes=32 * MIB),
        cost_estimate=pl.CostEstimate(
            flops=2 * EACH * 1024 * 720 * 192, bytes_accessed=6000000, transcendentals=0
        ),
    )(mixed, table)


def joining_kernel(rows, out, rest, wide, lines):
    for a in range(LATS):
        wide[...] = rows[a].astype(jnp.float32)
        for k in range(LINES):
            one = wide[pl.ds(k, HALF, stride=LINES), :]
            lines[pl.ds(a * LINES + k, HALF, stride=LATS * LINES), :] = one
    made = lines[...].reshape(HALF, LATS * LINES, LANES).astype(BF)
    out[...] = made[:, :SPLIT]
    rest[...] = made[:, SPLIT:]


def join(rows):
    return pl.pallas_call(
        joining_kernel,
        out_shape=[
            jax.ShapeDtypeStruct((HALF, SPLIT, LANES), BF),
            jax.ShapeDtypeStruct((HALF, LATS * LINES - SPLIT, LANES), BF),
        ],
        scratch_shapes=[
            pltpu.VMEM((HALF * LINES, LANES), jnp.float32),
            pltpu.VMEM((HALF * LATS * LINES, LANES), jnp.float32),
        ],
        compiler_params=pltpu.CompilerParams(vmem_limit_bytes=10 * MIB),
    )(rows)


def output_kernel(table, *refs):
    out = refs[-1]

    def line(r, at):
        return r[at] if len(r.shape) == 3 else r[:, at].reshape(-1, LANES)

    for i in range(0, STEP, 2):
        both = [jnp.concatenate([line(r, i + k) for r in refs[:-1]], axis=0) for k in range(2)]
        both = jnp.concatenate(both, axis=1)
        made = jnp.dot(table[...], both, preferred_element_type=jnp.float32)
        made = made.astype(BF).T[:, :OUT_COLS]
        for k in range(2):
            for half in range(2):
                at = (2 * k + half) * OUT_ROWS
                out[half, i + k] = made[at : at + OUT_ROWS]


def to_longitudes(table, pieces):
    def spec(v):
        if v.ndim == 4:
            return pl.BlockSpec((v.shape[0], STEP, v.shape[2], LANES), lambda s: (0, s, 0, 0))
        return pl.BlockSpec((STEP, v.shape[1], LANES), lambda s: (s, 0, 0))

    out = pl.pallas_call(
        output_kernel,
        grid=(HALF // STEP,),
        in_specs=[pl.BlockSpec(table.shape, lambda s: (0, 0))] + [spec(v) for v in pieces],
        out_specs=pl.BlockSpec((2, STEP, OUT_ROWS, OUT_COLS), lambda s: (0, s, 0, 0)),
        out_shape=jax.ShapeDtypeStruct((2, HALF, OUT_ROWS, OUT_COLS), BF),
        compiler_params=pltpu.CompilerParams(vmem_limit_bytes=56 * MIB),
    )(table, *pieces)
    return out.reshape(CHAN, OUT_ROWS, OUT_COLS)


def lon_order(first, last):
    lon = lax.axis_index("lon")
    columns = [lon, (lon + 6) % 8, (lon + 2) % 8, (lon + 4) % 8, (lon + 4) % 8]
    half = (first + last) // 2
    ranges = [(first, last), (first, last), (first, last), (first, half), (half, last)]
    return [(c, *r) for c, r in zip(columns + [c ^ 1 for c in columns], ranges * 2)]


def gather_lon(v):
    def along(u, d):
        return lax.ppermute(u, "lon", [(i, (i + 2 * d) % 8) for i in range(8)])

    def across(u):
        return lax.ppermute(u, "lon", [(i, i ^ 1) for i in range(8)])

    half = v.shape[1] // 2
    right, left = along(v, 1), along(v, -1)
    far = [along(right[:, :half], 1), along(left[:, half:], -1)]
    pieces = [v, right, left] + far
    return pieces + [across(u) for u in pieces]


def local(coarse_field, forward_table, degree_mixing_weight, synthesis_weight_table):
    ftab = jnp.pad(forward_table, ((0, SLOTS - OWN), (0, 0), (0, 0)))
    ftab = ftab.reshape(LATS, EACH * ROWS, 720)
    ftab, coarse_field = lax.optimization_barrier((ftab, coarse_field))
    ftab = swap(ftab, "lat")

    lon = lax.axis_index("lon")
    row = jnp.arange(2 * LONS * SLOTS, dtype=jnp.int32)[:, None]
    slot = row % SLOTS
    ids = row // SLOTS % LONS * OWN + jnp.minimum(slot, OWN - 1)
    points = (lon * 180 + jnp.arange(180, dtype=jnp.int32))[None, :]
    factor = LON_IN ** (-0.5)
    waves_in = waves(ids, row // (SLOTS * LONS), slot < OWN, points, LON_IN, factor)
    spectrum = shares(waves_in, jnp.transpose(coarse_field, (1, 2, 0)))

    wtab = pack(jnp.transpose(synthesis_weight_table, (0, 2, 1)))
    spectrum, ftab, wtab, lon = lax.optimization_barrier((spectrum, ftab, wtab, lon))
    spectrum = lax.psum_scatter(spectrum, "lon", scatter_dimension=0)
    wtab = swap(wtab, "lat")
    ftab = ftab.reshape(LATS, EACH, ROWS, 720)
    spectrum = spectrum.reshape(ROWS, 2, LATS, EACH, CHAN)
    spectrum = jnp.transpose(spectrum, (2, 3, 1, 0, 4))
    spectrum = spectrum.reshape(LATS, 2 * EACH * ROWS, CHAN)
    ids, turns, real = [], [], []
    orders = [(column, 0, SPLIT) for column in range(LONS)]
    orders += lon_order(SPLIT, 2 * SLOTS)
    for column, first, last in orders:
        line = jnp.arange(first, last, dtype=jnp.int32)
        ids.append(column * OWN + jnp.minimum(line // 2, OWN - 1))
        turns.append(line % 2)
        real.append(line // 2 < OWN)
    ids, turns, real = (jnp.concatenate(v)[None, :] for v in (ids, turns, real))
    points = (lon * OUT_COLS + jnp.arange(WIDE, dtype=jnp.int32))[:, None]
    table = waves(ids, turns, real, points, LON_OUT, KEPT_ORDERS ** (-0.5))
    w = degree_mixing_weight
    turned = jnp.concatenate([-w[..., CHAN:], w[..., :CHAN]], axis=-1)
    both = jnp.concatenate([w, turned], axis=1)
    spectrum, wtab, table, both = lax.optimization_barrier((spectrum, wtab, table, both))
    spectrum = swap(spectrum, "lat").reshape(LATS, EACH, 2, ROWS, CHAN)
    spectrum = jnp.transpose(spectrum, (1, 0, 3, 2, 4)).reshape(EACH, 720, 2 * CHAN)

    coef = jnp.einsum("ajlq,jqn->ajln", ftab, spectrum, preferred_element_type=jnp.float32)
    coef = swap(coef.astype(BF), "lat").reshape(SLOTS, ROWS, 2 * CHAN)

    mixed = jnp.einsum("mlt,ltu->mlu", coef, both, preferred_element_type=jnp.float32)
    mixed = swap(mixed.astype(BF).reshape(LATS, EACH, ROWS, 2 * CHAN), "lat")
    mixed = jnp.transpose(mixed, (1, 0, 2, 3)).reshape(EACH, 720, 2 * CHAN)
    rows, rest = join(swap(synthesise(mixed, wtab), "lat"))
    pieces = [lax.all_gather(rows, "lon", axis=0)] + gather_lon(rest)

    return to_longitudes(table, pieces)


def solution(mesh):
    in_specs = (
        P(None, "lat", "lon"),
        P("lon", "lat", None),
        P("lat", None, None),
        P("lon", None, "lat"),
    )
    out_specs = P(None, "lat", "lon")
    return jax.shard_map(local, mesh=mesh, in_specs=in_specs, out_specs=out_specs, check_vma=False)
```

```python
import math

import jax
import jax.numpy as jnp
from jax import lax
from jax.experimental import pallas as pl
from jax.experimental.pallas import tpu as pltpu
from jax.sharding import PartitionSpec as P

CHAN = 96
KEPT_ORDERS = 368
LON_IN = 1440
LON_OUT = 3600
LATS = 16
LONS = 8
OWN = 46
SLOTS = 48
EACH = 3
ROWS = 45
LINES = 2 * EACH
SPLIT = 64
HALF = 48
OUT_ROWS = 64
OUT_COLS = 450
WIDE = 464
LANES = 128
PAIRED, EIGHTS, PACKED = 960, 1056, 1088
STEP = 16
MIB = 1024 * 1024
BF = jnp.bfloat16


def waves(order_ids, turn, valid, points, modulus, factor):
    phases = (order_ids * points + turn * (modulus // 4)) % modulus
    angles = 2.0 * math.pi / modulus * phases.astype(jnp.float32)
    return (jnp.cos(angles) * jnp.where(valid, factor, 0.0)).astype(BF)


def swap(x, axis):
    return lax.all_to_all(x, axis, split_axis=0, concat_axis=0, tiled=True)


def share_kernel(waves_in, field, out):
    for q in range(0, field.shape[0], 2):
        some = [field[k] for k in range(q, min(q + 2, field.shape[0]))]
        some = jnp.concatenate([jnp.pad(v, ((0, 0), (0, LANES - CHAN))) for v in some], axis=1)
        made = jnp.dot(waves_in[...], some, preferred_element_type=jnp.float32).astype(BF)
        for k in range(some.shape[1] // LANES):
            one = made[:, k * LANES : k * LANES + CHAN].reshape(2, LONS, SLOTS, CHAN)
            for r in range(2):
                out[:, q + k, r * SLOTS : (r + 1) * SLOTS] = one[r]


def shares(waves_in, field):
    step = 9
    return pl.pallas_call(
        share_kernel,
        grid=(ROWS // step,),
        in_specs=[
            pl.BlockSpec(waves_in.shape, lambda s: (0, 0)),
            pl.BlockSpec((step, 180, CHAN), lambda s: (s, 0, 0)),
        ],
        out_specs=pl.BlockSpec((LONS, step, 2 * SLOTS, CHAN), lambda s: (0, s, 0, 0)),
        out_shape=jax.ShapeDtypeStruct((LONS, ROWS, 2 * SLOTS, CHAN), BF),
        compiler_params=pltpu.CompilerParams(vmem_limit_bytes=16 * MIB),
    )(waves_in, field)


def packing_kernel(*refs):
    out = refs[-1]
    ends = []
    for k, table in enumerate(refs[:-1]):
        for t in range(5):
            at = (5 * k + t) * OUT_ROWS
            out[0, at : at + OUT_ROWS] = table[0, :, t * LANES : (t + 1) * LANES]
        rest = table[0, :, 640:704]
        at = PAIRED + k * 32
        out[0, at : at + 32] = jnp.concatenate([rest[:32], rest[32:]], axis=1)
        rest = table[0, :, 704:].astype(jnp.float32)
        ends.append(jnp.concatenate([rest[8 * g : 8 * g + 8] for g in range(8)], axis=1))
    ends.append(jnp.zeros((8, LANES), jnp.float32))
    out[0, EIGHTS:] = jnp.concatenate(ends, axis=0).astype(BF)

    @pl.when(pl.program_id(0) == LATS - 1)
    def _():
        for k in range(OWN - (LATS - 1) * EACH, EACH):
            out[0, 5 * k * OUT_ROWS : 5 * (k + 1) * OUT_ROWS] = jnp.zeros((5 * OUT_ROWS, LANES), BF)
            out[0, PAIRED + k * 32 : PAIRED + (k + 1) * 32] = jnp.zeros((32, LANES), BF)
        there = lax.broadcasted_iota(jnp.int32, (32, LANES), 0) < 8 * (OWN - (LATS - 1) * EACH)
        last = jnp.where(there, jnp.concatenate(ends, axis=0), 0.0)
        out[0, EIGHTS:] = last.astype(BF)


def pack(table):
    def spec(k):
        return pl.BlockSpec(
            (1, OUT_ROWS, 720), lambda a: (jnp.minimum(a * EACH + k, OWN - 1), 0, 0)
        )

    return pl.pallas_call(
        packing_kernel,
        grid=(LATS,),
        in_specs=[spec(k) for k in range(EACH)],
        out_specs=pl.BlockSpec((1, PACKED, LANES), lambda a: (a, 0, 0)),
        out_shape=jax.ShapeDtypeStruct((LATS, PACKED, LANES), BF),
        compiler_params=pltpu.CompilerParams(vmem_limit_bytes=10 * MIB),
    )(*[table] * EACH)


def unpack(table, k):
    parts = []
    for t in range(5):
        at = (5 * k + t) * OUT_ROWS
        parts.append(table[:, at : at + OUT_ROWS].reshape(LATS * OUT_ROWS, LANES))
    pairs = table[:, PAIRED + k * 32 : PAIRED + (k + 1) * 32]
    pairs = jnp.concatenate([pairs[:, :, :64], pairs[:, :, 64:]], axis=1)
    ends = table[:, EIGHTS:].astype(jnp.float32)[:, 8 * k : 8 * k + 8]
    ends = jnp.concatenate([ends[:, :, 16 * g : 16 * g + 16] for g in range(8)], axis=1)
    ends = ends.reshape(LATS * OUT_ROWS, 16).astype(BF)
    return jnp.concatenate(parts + [pairs.reshape(LATS * OUT_ROWS, 64), ends], axis=1)


def synthesis_kernel(mixed, table, rows, lines):
    made = []
    for k in range(EACH):
        made.append(jnp.dot(unpack(table, k), mixed[k], preferred_element_type=jnp.float32))
    for b in range(LATS):
        for k in range(EACH):
            one = made[k][b * OUT_ROWS : (b + 1) * OUT_ROWS].astype(BF).T.astype(jnp.float32)
            for r in range(2):
                low, high = one[r * CHAN : r * CHAN + HALF], one[r * CHAN + HALF : (r + 1) * CHAN]
                side = jnp.concatenate([low, high], axis=1)
                lines[pl.ds(2 * k + r, HALF, stride=LINES), :] = side
        rows[b] = lines[...].astype(BF)


def synthesise(mixed, table):
    return pl.pallas_call(
        synthesis_kernel,
        out_shape=jax.ShapeDtypeStruct((LATS, HALF * LINES, LANES), BF),
        scratch_shapes=[pltpu.VMEM((HALF * LINES, LANES), jnp.float32)],
        compiler_params=pltpu.CompilerParams(vmem_limit_bytes=32 * MIB),
        cost_estimate=pl.CostEstimate(
            flops=2 * EACH * 1024 * 720 * 192, bytes_accessed=6000000, transcendentals=0
        ),
    )(mixed, table)


def joining_kernel(rows, out, rest, wide, lines):
    for a in range(LATS):
        wide[...] = rows[a].astype(jnp.float32)
        for k in range(LINES):
            one = wide[pl.ds(k, HALF, stride=LINES), :]
            lines[pl.ds(a * LINES + k, HALF, stride=LATS * LINES), :] = one
    made = lines[...].reshape(HALF, LATS * LINES, LANES).astype(BF)
    out[...] = made[:, :SPLIT]
    rest[...] = made[:, SPLIT:]


def join(rows):
    return pl.pallas_call(
        joining_kernel,
        out_shape=[
            jax.ShapeDtypeStruct((HALF, SPLIT, LANES), BF),
            jax.ShapeDtypeStruct((HALF, LATS * LINES - SPLIT, LANES), BF),
        ],
        scratch_shapes=[
            pltpu.VMEM((HALF * LINES, LANES), jnp.float32),
            pltpu.VMEM((HALF * LATS * LINES, LANES), jnp.float32),
        ],
        compiler_params=pltpu.CompilerParams(vmem_limit_bytes=10 * MIB),
    )(rows)


def output_kernel(table, *refs):
    out = refs[-1]

    def line(r, at):
        return r[at] if len(r.shape) == 3 else r[:, at].reshape(-1, LANES)

    for i in range(0, STEP, 2):
        both = [jnp.concatenate([line(r, i + k) for r in refs[:-1]], axis=0) for k in range(2)]
        both = jnp.concatenate(both, axis=1)
        made = jnp.dot(table[...], both, preferred_element_type=jnp.float32)
        made = made.astype(BF).T[:, :OUT_COLS]
        for k in range(2):
            for half in range(2):
                at = (2 * k + half) * OUT_ROWS
                out[half, i + k] = made[at : at + OUT_ROWS]


def to_longitudes(table, pieces):
    def spec(v):
        if v.ndim == 4:
            return pl.BlockSpec((v.shape[0], STEP, v.shape[2], LANES), lambda s: (0, s, 0, 0))
        return pl.BlockSpec((STEP, v.shape[1], LANES), lambda s: (s, 0, 0))

    out = pl.pallas_call(
        output_kernel,
        grid=(HALF // STEP,),
        in_specs=[pl.BlockSpec(table.shape, lambda s: (0, 0))] + [spec(v) for v in pieces],
        out_specs=pl.BlockSpec((2, STEP, OUT_ROWS, OUT_COLS), lambda s: (0, s, 0, 0)),
        out_shape=jax.ShapeDtypeStruct((2, HALF, OUT_ROWS, OUT_COLS), BF),
        compiler_params=pltpu.CompilerParams(vmem_limit_bytes=56 * MIB),
    )(table, *pieces)
    return out.reshape(CHAN, OUT_ROWS, OUT_COLS)


def lon_order(first, last):
    lon = lax.axis_index("lon")
    columns = [lon, (lon + 6) % 8, (lon + 2) % 8, (lon + 4) % 8, (lon + 4) % 8]
    half = (first + last) // 2
    ranges = [(first, last), (first, last), (first, last), (first, half), (half, last)]
    return [(c, *r) for c, r in zip(columns + [c ^ 1 for c in columns], ranges * 2)]


def gather_lon(v):
    def along(u, d):
        return lax.ppermute(u, "lon", [(i, (i + 2 * d) % 8) for i in range(8)])

    def across(u):
        return lax.ppermute(u, "lon", [(i, i ^ 1) for i in range(8)])

    half = v.shape[1] // 2
    right, left = along(v, 1), along(v, -1)
    far = [along(right[:, :half], 1), along(left[:, half:], -1)]
    pieces = [v, right, left] + far
    return pieces + [across(u) for u in pieces]


def local(coarse_field, forward_table, degree_mixing_weight, synthesis_weight_table):
    ftab = jnp.pad(forward_table, ((0, SLOTS - OWN), (0, 0), (0, 0)))
    ftab = ftab.reshape(LATS, EACH * ROWS, 720)
    ftab, coarse_field = lax.optimization_barrier((ftab, coarse_field))
    ftab = swap(ftab, "lat")

    lon = lax.axis_index("lon")
    row = jnp.arange(2 * LONS * SLOTS, dtype=jnp.int32)[:, None]
    slot = row % SLOTS
    ids = row // SLOTS % LONS * OWN + jnp.minimum(slot, OWN - 1)
    points = (lon * 180 + jnp.arange(180, dtype=jnp.int32))[None, :]
    factor = LON_IN ** (-0.5)
    waves_in = waves(ids, row // (SLOTS * LONS), slot < OWN, points, LON_IN, factor)
    spectrum = shares(waves_in, jnp.transpose(coarse_field, (1, 2, 0)))

    wtab = pack(jnp.transpose(synthesis_weight_table, (0, 2, 1)))
    spectrum, ftab, wtab, lon = lax.optimization_barrier((spectrum, ftab, wtab, lon))
    spectrum = lax.psum_scatter(spectrum, "lon", scatter_dimension=0)
    wtab = swap(wtab, "lat")
    ftab = ftab.reshape(LATS, EACH, ROWS, 720)
    spectrum = spectrum.reshape(ROWS, 2, LATS, EACH, CHAN)
    spectrum = jnp.transpose(spectrum, (2, 3, 1, 0, 4))
    spectrum = spectrum.reshape(LATS, 2 * EACH * ROWS, CHAN)
    ids, turns, real = [], [], []
    orders = [(column, 0, SPLIT) for column in range(LONS)]
    orders += lon_order(SPLIT, 2 * SLOTS)
    for column, first, last in orders:
        line = jnp.arange(first, last, dtype=jnp.int32)
        ids.append(column * OWN + jnp.minimum(line // 2, OWN - 1))
        turns.append(line % 2)
        real.append(line // 2 < OWN)
    ids, turns, real = (jnp.concatenate(v)[None, :] for v in (ids, turns, real))
    points = (lon * OUT_COLS + jnp.arange(WIDE, dtype=jnp.int32))[:, None]
    table = waves(ids, turns, real, points, LON_OUT, KEPT_ORDERS ** (-0.5))
    w = degree_mixing_weight
    turned = jnp.concatenate([-w[..., CHAN:], w[..., :CHAN]], axis=-1)
    both = jnp.concatenate([w, turned], axis=1)
    spectrum, wtab, ftab, table, both = lax.optimization_barrier(
        (spectrum, wtab, ftab, table, both)
    )
    spectrum = swap(spectrum, "lat").reshape(LATS, EACH, 2, ROWS, CHAN)
    spectrum = jnp.transpose(spectrum, (1, 0, 3, 2, 4)).reshape(EACH, 720, 2 * CHAN)

    coef = jnp.einsum("ajlq,jqn->ajln", ftab, spectrum, preferred_element_type=jnp.float32)
    coef = swap(coef.astype(BF), "lat").reshape(SLOTS, ROWS, 2 * CHAN)

    mixed = jnp.einsum("mlt,ltu->mlu", coef, both, preferred_element_type=jnp.float32)
    mixed = swap(mixed.astype(BF).reshape(LATS, EACH, ROWS, 2 * CHAN), "lat")
    mixed = jnp.transpose(mixed, (1, 0, 2, 3)).reshape(EACH, 720, 2 * CHAN)
    rows, rest = join(swap(synthesise(mixed, wtab), "lat"))
    pieces = [lax.all_gather(rows, "lon", axis=0)] + gather_lon(rest)

    return to_longitudes(table, pieces)


def solution(mesh):
    in_specs = (
        P(None, "lat", "lon"),
        P("lon", "lat", None),
        P("lat", None, None),
        P("lon", None, "lat"),
    )
    out_specs = P(None, "lat", "lon")
    return jax.shard_map(local, mesh=mesh, in_specs=in_specs, out_specs=out_specs, check_vma=False)
```

```python
import math

import jax
import jax.numpy as jnp
from jax import lax
from jax.experimental import pallas as pl
from jax.experimental.pallas import tpu as pltpu
from jax.sharding import PartitionSpec as P

CHAN = 96
KEPT_ORDERS = 368
LON_IN = 1440
LON_OUT = 3600
LATS = 16
LONS = 8
OWN = 46
SLOTS = 48
EACH = 3
ROWS = 45
LINES = 2 * EACH
SPLIT = 64
HALF = 48
OUT_ROWS = 64
OUT_COLS = 450
WIDE = 464
LANES = 128
PAIRED, EIGHTS, PACKED = 960, 1056, 1088
STEP = 16
MIB = 1024 * 1024
BF = jnp.bfloat16


def waves(order_ids, turn, valid, points, modulus, factor):
    phases = (order_ids * points + turn * (modulus // 4)) % modulus
    angles = 2.0 * math.pi / modulus * phases.astype(jnp.float32)
    return (jnp.cos(angles) * jnp.where(valid, factor, 0.0)).astype(BF)


def swap(x, axis):
    return lax.all_to_all(x, axis, split_axis=0, concat_axis=0, tiled=True)


def share_kernel(waves_in, field, out):
    for q in range(0, field.shape[0], 2):
        some = [field[k] for k in range(q, min(q + 2, field.shape[0]))]
        some = jnp.concatenate([jnp.pad(v, ((0, 0), (0, LANES - CHAN))) for v in some], axis=1)
        made = jnp.dot(waves_in[...], some, preferred_element_type=jnp.float32).astype(BF)
        for k in range(some.shape[1] // LANES):
            one = made[:, k * LANES : k * LANES + CHAN].reshape(2, LONS, SLOTS, CHAN)
            for r in range(2):
                out[:, q + k, r * SLOTS : (r + 1) * SLOTS] = one[r]


def shares(waves_in, field):
    step = 9
    return pl.pallas_call(
        share_kernel,
        grid=(ROWS // step,),
        in_specs=[
            pl.BlockSpec(waves_in.shape, lambda s: (0, 0)),
            pl.BlockSpec((step, 180, CHAN), lambda s: (s, 0, 0)),
        ],
        out_specs=pl.BlockSpec((LONS, step, 2 * SLOTS, CHAN), lambda s: (0, s, 0, 0)),
        out_shape=jax.ShapeDtypeStruct((LONS, ROWS, 2 * SLOTS, CHAN), BF),
        compiler_params=pltpu.CompilerParams(vmem_limit_bytes=16 * MIB),
    )(waves_in, field)


def packing_kernel(*refs):
    out = refs[-1]
    ends = []
    for k, table in enumerate(refs[:-1]):
        for t in range(5):
            at = (5 * k + t) * OUT_ROWS
            out[0, at : at + OUT_ROWS] = table[0, :, t * LANES : (t + 1) * LANES]
        rest = table[0, :, 640:704]
        at = PAIRED + k * 32
        out[0, at : at + 32] = jnp.concatenate([rest[:32], rest[32:]], axis=1)
        rest = table[0, :, 704:].astype(jnp.float32)
        ends.append(jnp.concatenate([rest[8 * g : 8 * g + 8] for g in range(8)], axis=1))
    ends.append(jnp.zeros((8, LANES), jnp.float32))
    out[0, EIGHTS:] = jnp.concatenate(ends, axis=0).astype(BF)

    @pl.when(pl.program_id(0) == LATS - 1)
    def _():
        for k in range(OWN - (LATS - 1) * EACH, EACH):
            out[0, 5 * k * OUT_ROWS : 5 * (k + 1) * OUT_ROWS] = jnp.zeros((5 * OUT_ROWS, LANES), BF)
            out[0, PAIRED + k * 32 : PAIRED + (k + 1) * 32] = jnp.zeros((32, LANES), BF)
        there = lax.broadcasted_iota(jnp.int32, (32, LANES), 0) < 8 * (OWN - (LATS - 1) * EACH)
        last = jnp.where(there, jnp.concatenate(ends, axis=0), 0.0)
        out[0, EIGHTS:] = last.astype(BF)


def pack(table):
    def spec(k):
        return pl.BlockSpec(
            (1, OUT_ROWS, 720), lambda a: (jnp.minimum(a * EACH + k, OWN - 1), 0, 0)
        )

    return pl.pallas_call(
        packing_kernel,
        grid=(LATS,),
        in_specs=[spec(k) for k in range(EACH)],
        out_specs=pl.BlockSpec((1, PACKED, LANES), lambda a: (a, 0, 0)),
        out_shape=jax.ShapeDtypeStruct((LATS, PACKED, LANES), BF),
        compiler_params=pltpu.CompilerParams(vmem_limit_bytes=10 * MIB),
    )(*[table] * EACH)


def unpack(table, k):
    parts = []
    for t in range(5):
        at = (5 * k + t) * OUT_ROWS
        parts.append(table[:, at : at + OUT_ROWS].reshape(LATS * OUT_ROWS, LANES))
    pairs = table[:, PAIRED + k * 32 : PAIRED + (k + 1) * 32]
    pairs = jnp.concatenate([pairs[:, :, :64], pairs[:, :, 64:]], axis=1)
    ends = table[:, EIGHTS:].astype(jnp.float32)[:, 8 * k : 8 * k + 8]
    ends = jnp.concatenate([ends[:, :, 16 * g : 16 * g + 16] for g in range(8)], axis=1)
    ends = ends.reshape(LATS * OUT_ROWS, 16).astype(BF)
    return jnp.concatenate(parts + [pairs.reshape(LATS * OUT_ROWS, 64), ends], axis=1)


def synthesis_kernel(mixed, table, rows, lines):
    made = []
    for k in range(EACH):
        made.append(jnp.dot(unpack(table, k), mixed[k], preferred_element_type=jnp.float32))
    for b in range(LATS):
        for k in range(EACH):
            one = made[k][b * OUT_ROWS : (b + 1) * OUT_ROWS].astype(BF).T.astype(jnp.float32)
            for r in range(2):
                low, high = one[r * CHAN : r * CHAN + HALF], one[r * CHAN + HALF : (r + 1) * CHAN]
                side = jnp.concatenate([low, high], axis=1)
                lines[pl.ds(2 * k + r, HALF, stride=LINES), :] = side
        rows[b] = lines[...].astype(BF)


def synthesise(mixed, table):
    return pl.pallas_call(
        synthesis_kernel,
        out_shape=jax.ShapeDtypeStruct((LATS, HALF * LINES, LANES), BF),
        scratch_shapes=[pltpu.VMEM((HALF * LINES, LANES), jnp.float32)],
        compiler_params=pltpu.CompilerParams(vmem_limit_bytes=32 * MIB),
        cost_estimate=pl.CostEstimate(
            flops=2 * EACH * 1024 * 720 * 192, bytes_accessed=6000000, transcendentals=0
        ),
    )(mixed, table)


def joining_kernel(rows, out, rest, wide, lines):
    for a in range(LATS):
        wide[...] = rows[a].astype(jnp.float32)
        for k in range(LINES):
            one = wide[pl.ds(k, HALF, stride=LINES), :]
            lines[pl.ds(a * LINES + k, HALF, stride=LATS * LINES), :] = one
    made = lines[...].reshape(HALF, LATS * LINES, LANES).astype(BF)
    out[...] = made[:, :SPLIT]
    rest[...] = made[:, SPLIT:]


def join(rows):
    return pl.pallas_call(
        joining_kernel,
        out_shape=[
            jax.ShapeDtypeStruct((HALF, SPLIT, LANES), BF),
            jax.ShapeDtypeStruct((HALF, LATS * LINES - SPLIT, LANES), BF),
        ],
        scratch_shapes=[
            pltpu.VMEM((HALF * LINES, LANES), jnp.float32),
            pltpu.VMEM((HALF * LATS * LINES, LANES), jnp.float32),
        ],
        compiler_params=pltpu.CompilerParams(vmem_limit_bytes=10 * MIB),
    )(rows)


def output_kernel(table, *refs):
    out = refs[-1]

    def line(r, at):
        return r[at] if len(r.shape) == 3 else r[:, at].reshape(-1, LANES)

    for i in range(0, STEP, 2):
        both = [jnp.concatenate([line(r, i + k) for r in refs[:-1]], axis=0) for k in range(2)]
        both = jnp.concatenate(both, axis=1)
        made = jnp.dot(table[...], both, preferred_element_type=jnp.float32)
        made = made.astype(BF).T[:, :OUT_COLS]
        for k in range(2):
            for half in range(2):
                at = (2 * k + half) * OUT_ROWS
                out[half, i + k] = made[at : at + OUT_ROWS]


def to_longitudes(table, pieces):
    def spec(v):
        if v.ndim == 4:
            return pl.BlockSpec((v.shape[0], STEP, v.shape[2], LANES), lambda s: (0, s, 0, 0))
        return pl.BlockSpec((STEP, v.shape[1], LANES), lambda s: (s, 0, 0))

    out = pl.pallas_call(
        output_kernel,
        grid=(HALF // STEP,),
        in_specs=[pl.BlockSpec(table.shape, lambda s: (0, 0))] + [spec(v) for v in pieces],
        out_specs=pl.BlockSpec((2, STEP, OUT_ROWS, OUT_COLS), lambda s: (0, s, 0, 0)),
        out_shape=jax.ShapeDtypeStruct((2, HALF, OUT_ROWS, OUT_COLS), BF),
        compiler_params=pltpu.CompilerParams(vmem_limit_bytes=56 * MIB),
    )(table, *pieces)
    return out.reshape(CHAN, OUT_ROWS, OUT_COLS)


def lon_order(first, last):
    lon = lax.axis_index("lon")
    columns = [lon, (lon + 6) % 8, (lon + 2) % 8, (lon + 4) % 8, (lon + 4) % 8]
    half = (first + last) // 2
    ranges = [(first, last), (first, last), (first, last), (first, half), (half, last)]
    return [(c, *r) for c, r in zip(columns + [c ^ 1 for c in columns], ranges * 2)]


def gather_lon(v):
    def along(u, d):
        return lax.ppermute(u, "lon", [(i, (i + 2 * d) % 8) for i in range(8)])

    def across(u):
        return lax.ppermute(u, "lon", [(i, i ^ 1) for i in range(8)])

    half = v.shape[1] // 2
    right, left = along(v, 1), along(v, -1)
    far = [along(right[:, :half], 1), along(left[:, half:], -1)]
    pieces = [v, right, left] + far
    return pieces + [across(u) for u in pieces]


def local(coarse_field, forward_table, degree_mixing_weight, synthesis_weight_table):
    ftab = jnp.pad(forward_table, ((0, SLOTS - OWN), (0, 0), (0, 0)))
    ftab = ftab.reshape(LATS, EACH * ROWS, 720)
    ftab, coarse_field = lax.optimization_barrier((ftab, coarse_field))
    ftab = swap(ftab, "lat")

    lon = lax.axis_index("lon")
    row = jnp.arange(2 * LONS * SLOTS, dtype=jnp.int32)[:, None]
    slot = row % SLOTS
    ids = row // SLOTS % LONS * OWN + jnp.minimum(slot, OWN - 1)
    points = (lon * 180 + jnp.arange(180, dtype=jnp.int32))[None, :]
    factor = LON_IN ** (-0.5)
    waves_in = waves(ids, row // (SLOTS * LONS), slot < OWN, points, LON_IN, factor)
    spectrum = shares(waves_in, jnp.transpose(coarse_field, (1, 2, 0)))

    wtab = pack(jnp.transpose(synthesis_weight_table, (0, 2, 1)))
    spectrum, ftab, wtab, lon = lax.optimization_barrier((spectrum, ftab, wtab, lon))
    spectrum = lax.psum_scatter(spectrum, "lon", scatter_dimension=0)
    wtab = swap(wtab, "lat")
    ftab = ftab.reshape(LATS, EACH, ROWS, 720)
    spectrum = spectrum.reshape(ROWS, 2, LATS, EACH, CHAN)
    spectrum = jnp.transpose(spectrum, (2, 3, 1, 0, 4))
    spectrum = spectrum.reshape(LATS, 2 * EACH * ROWS, CHAN)
    ids, turns, real = [], [], []
    orders = [(column, 0, SPLIT) for column in range(LONS)]
    orders += lon_order(SPLIT, 2 * SLOTS)
    for column, first, last in orders:
        line = jnp.arange(first, last, dtype=jnp.int32)
        ids.append(column * OWN + jnp.minimum(line // 2, OWN - 1))
        turns.append(line % 2)
        real.append(line // 2 < OWN)
    ids, turns, real = (jnp.concatenate(v)[None, :] for v in (ids, turns, real))
    points = (lon * OUT_COLS + jnp.arange(WIDE, dtype=jnp.int32))[:, None]
    table = waves(ids, turns, real, points, LON_OUT, KEPT_ORDERS ** (-0.5))
    w = degree_mixing_weight
    turned = jnp.concatenate([-w[..., CHAN:], w[..., :CHAN]], axis=-1)
    both = jnp.concatenate([w, turned], axis=1)
    spectrum, wtab, ftab, table, both = lax.optimization_barrier(
        (spectrum, wtab, ftab, table, both)
    )
    spectrum = swap(spectrum, "lat").reshape(LATS, EACH, 2, ROWS, CHAN)
    spectrum = jnp.transpose(spectrum, (1, 0, 3, 2, 4)).reshape(EACH, 720, 2 * CHAN)

    coef = jnp.einsum("ajlq,jqn->ajln", ftab, spectrum, preferred_element_type=jnp.float32)
    coef = coef.astype(BF).reshape(LATS, EACH * ROWS, 2 * CHAN)
    coef = swap(coef, "lat").reshape(SLOTS, ROWS, 2 * CHAN)

    mixed = jnp.einsum("mlt,ltu->mlu", coef, both, preferred_element_type=jnp.float32)
    mixed = swap(mixed.astype(BF).reshape(LATS, EACH, ROWS, 2 * CHAN), "lat")
    mixed = jnp.transpose(mixed, (1, 0, 2, 3)).reshape(EACH, 720, 2 * CHAN)
    rows, rest = join(swap(synthesise(mixed, wtab), "lat"))
    pieces = [lax.all_gather(rows, "lon", axis=0)] + gather_lon(rest)

    return to_longitudes(table, pieces)


def solution(mesh):
    in_specs = (
        P(None, "lat", "lon"),
        P("lon", "lat", None),
        P("lat", None, None),
        P("lon", None, "lat"),
    )
    out_specs = P(None, "lat", "lon")
    return jax.shard_map(local, mesh=mesh, in_specs=in_specs, out_specs=out_specs, check_vma=False)
```
